256 devices in a mesh: gx: 32 (over y, z_lo, core), gy: 8 (over z_hi, x).
Axes of the slice: x: 4, y: 4, z: 8 (z_hi: 2, z_lo: 4; z = z_hi * 4 + z_lo), core: 2. Of those that a mesh axis runs over, the one named last changes fastest.
Arguments:
- c_start: float32 [12, 32, 16, 1024], P(None, 'gx', None, 'gy'), may hold values from -6 to 6
- log_tort: float32 [32, 16, 1024], P('gx', None, 'gy'), may hold values from -0.7 to 0.7
- direction: float32 [32, 16, 1024], P('gx', None, 'gy'), may hold values from -3 to 5
- mix_inverse: float32 [4, 12, 12], replicated, may hold values from -0.055 to 1
- pair_mask: int32 [12, 12], replicated, may hold values 0 or 1
- soil_layer: int32 [32, 1024], P('gx', 'gy'), may hold values from 0 to 3
- observed: float32 [12, 32, 1024], P(None, 'gx', 'gy'), may hold values from -9 to 9
Outputs:
- hess_vec: float32 [32, 16, 1024], P('gx', None, 'gy')
The draws below stay inside these ranges and needn't reach their ends.
All inputs are finite; a program needn't handle non-finite values.
Results may differ from the reference program's by a relative error of at most 0.00014.
Values sent between devices are 32-bit elements; how exact they have to be, the bound alone decides.
A program may use at most 64 MiB of HBM per device.

```python
import jax
import jax.numpy as jnp
from jax import lax

SPECIES = 12
LAYERS = 4
NZ = 16
STEPS = 3
NX = 32
NY = 1024
NOBS = 393216


def draw_direction(key, part):
    key = jax.random.fold_in(key, 37)
    first, second = jax.random.split(key)
    level = jax.random.uniform(first, (), jnp.float32, 0.8, 1.5)
    values = jax.random.truncated_normal(second, -3.0, 3.0, (NX, NZ, NY), jnp.float32) * 0.75 + level
    return values.astype(jnp.float32)


def draw_mix_inverse(key, part):
    key = jax.random.fold_in(key, 11)
    first, second = jax.random.split(key)
    diagonal = jax.random.uniform(first, (LAYERS, SPECIES), jnp.float32, 0.7, 1.0)
    offdiag = jax.random.uniform(second, (LAYERS, SPECIES, SPECIES), jnp.float32, -0.05, 0.05)
    unit = (lax.broadcasted_iota(jnp.int32, (SPECIES, SPECIES), 0) == lax.broadcasted_iota(jnp.int32, (SPECIES, SPECIES), 1)).astype(jnp.float32)
    return offdiag * (1.0 - unit)[None] + unit[None] * diagonal[:, :, None]


def draw_observed(key, part):
    key = jax.random.fold_in(key, 23)
    rising = 1.0 + 2.0 * lax.broadcasted_iota(jnp.float32, (SPECIES, NX, NY), 1) / NX
    values = jax.random.truncated_normal(key, -3.0, 3.0, (SPECIES, NX, NY), jnp.float32) * rising
    return values.astype(jnp.float32)


def set_ends(values, rng, smallest, high):
    longest = values.shape.index(max(values.shape))
    spots = []
    for shift in (0, 1):
        where = [jax.random.randint(jax.random.fold_in(rng, axis), (), 0, length) for axis, length in enumerate(values.shape)]
        where[longest] = (where[longest] + shift) % values.shape[longest]
        spots.append(tuple(where))
    return values.at[spots[0]].set(smallest).at[spots[1]].set(high)


def shard_levels(rng, dims, cuts, low, top_value):
    def one(axis_at, parts):
        heights = jax.random.uniform(jax.random.fold_in(jax.random.fold_in(rng, 6), axis_at), (parts,), jnp.float32, low / len(cuts), top_value / len(cuts))
        return jnp.repeat(jnp.exp(heights), dims[axis_at] // parts).reshape((-1,) + (1,) * (len(dims) - axis_at - 1))

    gain = one(*cuts[0])
    for cut in cuts[1:]:
        gain = gain * one(*cut)
    return gain


def scatter_about(own_key, dims, scale, most, shards=(), kind=jnp.bfloat16):
    values = scale * jax.random.normal(own_key, dims, jnp.float32)
    if shards:
        values = values * shard_levels(own_key, dims, shards, -0.22, 0.18)
    return jnp.clip(values, -most, most).astype(kind)


def setup_inputs(seed: int = 0) -> dict:
    keys = jax.random.split(jax.random.key(seed), 8)
    c_start = scatter_about(keys[0], (SPECIES, NX, NZ, NY), 1.0, 6.0, ((1, 32), (3, 8)), jnp.float32)
    log_tort = jnp.clip(jax.random.uniform(keys[1], (NX, NZ, NY), jnp.float32, -0.7, 0.7) * shard_levels(keys[1], (NX, NZ, NY), ((0, 32), (2, 8)), -0.4, 0.0), -0.7, 0.7)
    direction = draw_direction(jax.random.fold_in(keys[7], 71), 0)
    mix_inverse = draw_mix_inverse(jax.random.fold_in(keys[7], 71), 0)
    pair_mask = set_ends((jax.random.randint(keys[4], (SPECIES, SPECIES), 0, 2) < 1).astype(jnp.int32), jax.random.fold_in(keys[4], 1), 0, 1)
    soil_layer = set_ends(jax.random.randint(keys[5], (NX, NY), 0, LAYERS), jax.random.fold_in(keys[5], 1), 0, LAYERS - 1).astype(jnp.int32)
    observed = draw_observed(jax.random.fold_in(keys[7], 71), 0)
    return {"c_start": c_start, "log_tort": log_tort, "direction": direction, "mix_inverse": mix_inverse, "pair_mask": pair_mask, "soil_layer": soil_layer, "observed": observed}


DT = 0.04
NEIGHBOURS = ((1, 0, 0), (-1, 0, 0), (0, 1, 0), (0, -1, 0), (0, 0, 1), (0, 0, -1))

def window(array, shift_x, shift_z, shift_y):
    extent = array.shape[-3:]
    return array[..., 1 + shift_x:extent[0] - 1 + shift_x, 1 + shift_z:extent[1] - 1 + shift_z, 1 + shift_y:extent[2] - 1 + shift_y]

def advance(state_pad, tort_pad, mixers, masks):
    coeff = jnp.exp(tort_pad)
    center = window(state_pad, 0, 0, 0)
    middle = window(coeff, 0, 0, 0)
    spread = jnp.zeros_like(center)
    for shift_x, shift_z, shift_y in NEIGHBOURS:
        face = 0.5 * (middle + window(coeff, shift_x, shift_z, shift_y))
        spread = spread + face * (window(state_pad, shift_x, shift_z, shift_y) - center)
    mixed = jnp.zeros_like(center)
    for level in range(mixers.shape[0]):
        mixed = mixed + masks[level] * jnp.einsum('st,txzy->sxzy', mixers[level], spread, precision=lax.Precision.HIGHEST)
    return center + DT * mixed

def effective_mixers(mix_inverse, pair_mask):
    count = mix_inverse.shape[1]
    diagonal = lax.broadcasted_iota(jnp.int32, (count, count), 0) == lax.broadcasted_iota(jnp.int32, (count, count), 1)
    return jnp.where(diagonal[None], mix_inverse, mix_inverse * pair_mask.astype(jnp.float32)[None])

def layer_masks(soil_layer, levels):
    return (soil_layer[None, :, None, :] == jnp.arange(levels, dtype=jnp.int32)[:, None, None, None]).astype(jnp.float32)

def reference(c_start, log_tort, direction, mix_inverse, pair_mask, soil_layer, observed):
    mixers = effective_mixers(mix_inverse, pair_mask)
    masks = layer_masks(soil_layer, LAYERS)

    def misfit(tortuosity):
        tort_pad = jnp.pad(tortuosity, 1)
        state = c_start
        for moment in range(STEPS):
            state = advance(jnp.pad(state, ((0, 0), (1, 1), (1, 1), (1, 1))), tort_pad, mixers, masks)
        mismatch = state[:, :, 0, :] - observed
        total = jnp.sum(mismatch * mismatch)
        return 0.5 * NOBS * jnp.log(total / NOBS)
    return jax.jvp(jax.grad(misfit), (log_tort,), (direction,))[1]
```

```python
import jax
import jax.numpy as jnp
from jax import lax
from jax.experimental import pallas as pl
from jax.experimental.pallas import tpu as pltpu
from jax.sharding import PartitionSpec as P

MESH = pl.DeviceIdType.MESH
DT = 0.04
STEPS = 3
SPECIES = 12
LAYERS = 4
LANES = 128
ROWS = 16
TORT, DIRE, SOIL = 12, 13, 14


def offsets():
    found = []
    for dx in range(-STEPS, STEPS + 1):
        for dy in (-1, 0, 1):
            depths = STEPS + 1 - abs(dx) - (1 if dy else 0)
            if depths > 0 and (dx or dy):
                found.append((dx, dy, depths))
    return found


ALONG_X = [(dx, dy, depths) for dx, dy, depths in offsets() if dy == 0]
ACROSS = [(dx, dy) for dx, dy, _ in offsets() if dy]
STRIP = {place: i for i, place in enumerate(ACROSS)}
HALO, HALO_ROWS = {}, 0
for dx, _, depths in ALONG_X:
    HALO[dx] = HALO_ROWS
    HALO_ROWS += depths * ROWS
RIM_ROWS = 24
RIM = {dx: i * RIM_ROWS for i, (dx, _, _) in enumerate(ALONG_X)}
FWD_MAIN = {dx: i for i, dx in enumerate(range(-2, 3))}
FWD_EDGE = {dx: 5 + i for i, dx in enumerate(range(-1, 2))}
ADJ_MAIN = {dx: i for i, dx in enumerate(range(-3, 4))}
ADJ_EDGE = {dx: 7 + i for i, dx in enumerate(range(-2, 3))}


def lane(shape):
    return lax.broadcasted_iota(jnp.int32, shape, len(shape) - 1)


def spin(value, by):
    return pltpu.roll(value, by % LANES, value.ndim - 1)


def y_next(main, edge):
    last = lane(main.shape) == LANES - 1
    a, b = spin(main, -1), spin(edge, -1)
    return jnp.where(last, b, a), jnp.where(last, a, b)


def y_prev(main, edge):
    first = lane(main.shape) == 0
    a, b = spin(main, 1), spin(edge, 1)
    return jnp.where(first, b, a), jnp.where(first, a, b)


def pack_strips(tiles):
    group = lane((8, LANES)) // 8
    packed = tiles[0]
    for i, tile in enumerate(tiles[1:], 1):
        packed = jnp.where(group == i, spin(tile, 8 * i), packed)
        packed = jnp.where(group == 15 - i, spin(tile, -8 * i), packed)
    return packed


def unpack_strip(left, right, i):
    return jnp.where(lane((8, LANES)) < LANES // 2, spin(right, -8 * i), spin(left, 8 * i))


def faces(main, edge, closed):
    out = {}
    for kind, field in (("m", main), ("e", edge)):
        for dx in field:
            value = field[dx]
            if dx + 1 in field:
                n = min(value.shape[0], field[dx + 1].shape[0])
                out["x" + kind, dx] = field[dx + 1][:n] - value[:n]
            parts = [value[:1]]
            if value.shape[0] > 1:
                parts.append(value[1:] - value[:-1])
            if closed:
                parts.append(-value[-1:])
            out["z" + kind, dx] = jnp.concatenate(parts, 0) if len(parts) > 1 else parts[0]
    for dx in edge:
        n = edge[dx].shape[0]
        a, b = y_next(main[dx][:n], edge[dx][:n])
        out["ym", dx] = a - main[dx][:n]
        out["ye", dx] = b - edge[dx][:n]
    return out


def times(coeff, diff):
    return {key: coeff[key][: diff[key].shape[0]] * diff[key] for key in diff}


def plus(one, two):
    return {key: one[key] + two[key] for key in one}


def gathered(flux, reach, closed):
    result = []
    for kind, most in (("m", reach), ("e", reach - 1)):
        field = {}
        for dx in range(-most, most + 1):
            depth = flux["z" + kind, dx]
            n = depth.shape[0] - 1
            total = depth[1:] - depth[:-1]
            a, b = y_prev(flux["ym", dx], flux["ye", dx])
            back = a if kind == "m" else b
            side = (
                flux["x" + kind, dx][:n]
                - flux["x" + kind, dx - 1][:n]
                + flux["y" + kind, dx][:n]
                - back[:n]
            )
            if closed:
                total = jnp.concatenate([total[:n] + side, -depth[n:]], 0)
            else:
                total = total + side
            field[dx] = total
        result.append(field)
    return result


def mixed(table, column, value):
    total = None
    for t in range(SPECIES):
        part = table[column, t] * value[:, t // 8 : t // 8 + 1, t % 8 : t % 8 + 1, :]
        total = part if total is None else total + part
    return total


def select_table(table, column, parts, soil):
    masks = [soil == float(level) for level in range(LAYERS)]
    for t in range(SPECIES):
        for half in range(2):
            value = jnp.zeros((8, LANES), jnp.float32)
            for level in range(LAYERS):
                value = jnp.where(masks[level], parts[level, t, half], value)
            table[column, t, half] = value


def kernel(
    nx, ny, c_hbm, m_hbm, d_hbm, mix_hbm, pair_hbm, soil_hbm, obs_hbm, out_ref,
    stage, soil_v, obs_v, mix_ref, pair_ref, block, strip, halo, halo_y, rim_out, rim_strip, rim, rim_y,
    part_out, part_a, part_b,
    square, fwd_parts, adj_parts, fwd, adj,
    local_sem, send_sem, recv_sem,
):
    x, y = lax.axis_index("gx"), lax.axis_index("gy")
    x_hi, x_mid, x_core = x // 8, (x // 2) % 4, x % 2
    y_hi, y_lo = y // 4, y % 4

    def at(dx, dy):
        return (x + dx + nx) % nx, (y + dy + ny) % ny

    group_a = []
    for i in range(1, 16):
        core, mid, high = i % 2, (i // 2) % 4, i // 8
        group_a.append((x_hi * 8 + (x_mid + mid) % 4 * 2 + (x_core + core) % 2, (y_hi + high) % 2 * 4 + y_lo))
    group_b = []
    for i in range(1, 16):
        low, high = i % 4, i // 4
        group_b.append(((x_hi + high) % 4 * 8 + x_mid * 2 + x_core, y_hi * 4 + (y_lo + low) % 4))

    loads = [
        pltpu.make_async_copy(c_hbm.at[:, 0, 0:8], stage.at[0:SPECIES], local_sem.at[0]),
        pltpu.make_async_copy(m_hbm.at[0, 0:8], stage.at[TORT], local_sem.at[1]),
        pltpu.make_async_copy(d_hbm.at[0, 0:8], stage.at[DIRE], local_sem.at[2]),
        pltpu.make_async_copy(soil_hbm, soil_v, local_sem.at[3]),
        pltpu.make_async_copy(mix_hbm, mix_ref, local_sem.at[4]),
        pltpu.make_async_copy(pair_hbm, pair_ref, local_sem.at[5]),
        pltpu.make_async_copy(obs_hbm, obs_v, local_sem.at[6]),
    ]
    for copy in loads:
        copy.start()
    barrier = pltpu.get_barrier_semaphore()
    partners = [at(dx, dy) for dx, dy, _ in offsets()] + group_a + group_b
    for partner in partners:
        pl.semaphore_signal(barrier, inc=1, device_id=partner, device_id_type=MESH)

    stage[SOIL] = jnp.zeros((8, LANES), jnp.float32)
    stage[SOIL + 1] = jnp.zeros((8, LANES), jnp.float32)
    for copy in loads[:4]:
        copy.wait()
    stage[SOIL, 0:1] = soil_v[...].astype(jnp.float32)
    flat = stage.reshape(ROWS * 8, LANES)
    for z in range(STEPS + 1):
        for half in range(2):
            block[pl.ds(z * ROWS + half * 8, 8)] = flat[pl.ds(half * 64 + z, 8, stride=8)]
    strip[...] = pack_strips([block[i * 8 : i * 8 + 8] for i in range(2 * STEPS)])

    pl.semaphore_wait(barrier, len(partners))

    def send(src, dst, number, partner):
        pltpu.make_async_remote_copy(
            src_ref=src, dst_ref=dst, send_sem=send_sem.at[number], recv_sem=recv_sem.at[number],
            device_id=partner, device_id_type=MESH,
        ).start()

    def received(buffer, number):
        pltpu.make_async_copy(buffer, buffer, recv_sem.at[number]).wait()

    def sent(buffer, number):
        pltpu.make_async_copy(buffer, buffer, send_sem.at[number]).wait()

    for dx, dy, depths in ALONG_X:
        rows = depths * ROWS
        send(block.at[pl.ds(0, rows)], halo.at[pl.ds(HALO[-dx], rows)], 0, at(dx, dy))
    for dx, dy in ACROSS:
        send(strip, halo_y.at[STRIP[-dx, -dy]], 1, at(dx, dy))

    for copy in loads[4:]:
        copy.wait()
    square[...] = jnp.zeros((LANES, LANES), jnp.float32)
    diagonal = lax.broadcasted_iota(jnp.int32, (SPECIES, SPECIES), 0) == lax.broadcasted_iota(
        jnp.int32, (SPECIES, SPECIES), 1
    )
    pair = pair_ref[...].astype(jnp.float32)
    for level in range(LAYERS):
        entry = mix_ref[:, level, :]
        square[level * ROWS : level * ROWS + SPECIES, 0:SPECIES] = jnp.where(diagonal, entry, entry * pair)
    plain = square[...]
    turned = plain.T
    for level in range(LAYERS):
        for t in range(SPECIES):
            for half in range(2):
                row = level * ROWS + half * 8
                fwd_parts[level, t, half] = jnp.broadcast_to(plain[row : row + 8, t : t + 1], (8, LANES))
                col = level * ROWS + t
                adj_parts[level, t, half] = jnp.broadcast_to(
                    turned[half * 8 : half * 8 + 8, col : col + 1], (8, LANES)
                )

    received(halo, 0)
    received(halo_y, 1)

    in_x = {dx: jnp.logical_and(x + dx >= 0, x + dx < nx) for dx in range(-STEPS, STEPS + 1)}
    species_row = lax.broadcasted_iota(jnp.int32, (1, 2, 8, LANES), 1) * 8 + lax.broadcasted_iota(
        jnp.int32, (1, 2, 8, LANES), 2
    )
    right_half = lane((8, LANES)) < LANES // 2
    in_y = jnp.where(right_half, y + 1, y - 1)
    in_y = jnp.logical_and(in_y >= 0, in_y < ny)

    def cells(ref, start, depths):
        return ref[pl.ds(start, depths * ROWS)].reshape(depths, 2, 8, LANES)

    def row_of(value, row):
        depths = value.shape[0]
        return jnp.broadcast_to(value[:, row // 8, row % 8 : row % 8 + 1, :], (depths, 8, LANES))

    def zero_unless(valid, value):
        return jnp.where(jnp.broadcast_to(valid, value.shape), value, 0.0)

    def unpack(value, valid):
        depths = value.shape[0]
        state = jnp.where(jnp.broadcast_to(species_row < SPECIES, value.shape), value, 0.0)
        tort, dire = row_of(value, TORT), row_of(value, DIRE)
        soil = row_of(value[:1], SOIL)[0]
        if valid is not None:
            state = zero_unless(valid, state)
            tort, dire = zero_unless(valid, tort), zero_unless(valid, dire)
            soil = jnp.where(valid, soil, -1.0)
        weight = (0.5 * DT) * jnp.exp(tort)
        turn = weight * dire
        shape = (depths, 1, 8, LANES)
        return state, weight.reshape(shape), turn.reshape(shape), dire.reshape(shape), soil

    main, edge = {}, {}
    weight_m, weight_e, turn_m, turn_e, soil_m, soil_e = {}, {}, {}, {}, {}, {}
    for dx in range(-STEPS, STEPS + 1):
        depths = STEPS + 1 - abs(dx)
        raw = cells(block, 0, depths) if dx == 0 else cells(halo, HALO[dx], depths)
        valid = None if dx == 0 else jnp.broadcast_to(in_x[dx], (8, LANES))
        main[dx], weight_m[dx], turn_m[dx], dire, soil_m[dx] = unpack(raw, valid)
        if dx == 0:
            own_dire = dire
        if abs(dx) < STEPS:
            left, right = halo_y[STRIP[dx, -1]], halo_y[STRIP[dx, 1]]
            raw = jnp.stack([unpack_strip(left, right, i) for i in range(2 * (depths - 1))])
            raw = raw.reshape(depths - 1, 2, 8, LANES)
            valid = jnp.logical_and(in_y, jnp.broadcast_to(in_x[dx], (8, LANES)))
            edge[dx], weight_e[dx], turn_e[dx], _, soil_e[dx] = unpack(raw, valid)

    def face_sums(main_w, edge_w, outside):
        out = {}
        for kind, field in (("m", main_w), ("e", edge_w)):
            for dx in field:
                value = field[dx]
                if dx + 1 in field:
                    n = min(value.shape[0], field[dx + 1].shape[0])
                    out["x" + kind, dx] = field[dx + 1][:n] + value[:n]
                parts = [value[:1] + outside]
                if value.shape[0] > 1:
                    parts.append(value[1:] + value[:-1])
                out["z" + kind, dx] = jnp.concatenate(parts, 0) if len(parts) > 1 else parts[0]
        for dx in edge_w:
            n = edge_w[dx].shape[0]
            a, b = y_next(main_w[dx][:n], edge_w[dx][:n])
            out["ym", dx] = a + main_w[dx][:n]
            out["ye", dx] = b + edge_w[dx][:n]
        return out

    coeff = face_sums(weight_m, weight_e, 0.5 * DT)
    slope = face_sums(turn_m, turn_e, 0.0)

    for dx, column in FWD_MAIN.items():
        select_table(fwd, column, fwd_parts, soil_m[dx])
    for dx, column in FWD_EDGE.items():
        select_table(fwd, column, fwd_parts, soil_e[dx])

    diffs, diffs_dot = [], []
    main_dot, edge_dot = None, None
    for k in range(STEPS):
        reach = STEPS - 1 - k
        diff = faces(main, edge, False)
        diffs.append(diff)
        flux = times(coeff, diff)
        flux_dot = times(slope, diff)
        if main_dot is not None:
            diff_dot = faces(main_dot, edge_dot, False)
            flux_dot = plus(flux_dot, times(coeff, diff_dot))
        else:
            diff_dot = None
        diffs_dot.append(diff_dot)
        spread_m, spread_e = gathered(flux, reach, False)
        dot_m, dot_e = gathered(flux_dot, reach, False)
        new = [{}, {}, {}, {}]
        for kind, table, old, old_dot, spread, dot in (
            (0, FWD_MAIN, main, main_dot, spread_m, dot_m),
            (1, FWD_EDGE, edge, edge_dot, spread_e, dot_e),
        ):
            for dx in spread:
                n = spread[dx].shape[0]
                new[kind][dx] = old[dx][:n] + mixed(fwd, table[dx], spread[dx])
                moved = mixed(fwd, table[dx], dot[dx])
                new[2 + kind][dx] = moved if old_dot is None else old_dot[dx][:n] + moved
        main, edge, main_dot, edge_dot = new

    obs = jnp.concatenate([obs_v[s] for s in range(SPECIES)] + [jnp.zeros((ROWS - SPECIES, LANES), jnp.float32)], 0)
    miss = main[0].reshape(ROWS, LANES) - obs
    miss_dot = main_dot[0].reshape(ROWS, LANES)
    square_sum = jnp.sum(miss * miss, 0, keepdims=True)
    cross_sum = jnp.sum(miss * miss_dot, 0, keepdims=True)
    front = lane((1, LANES)) < LANES // 2
    half_row = LANES // 2
    part = jnp.where(front, square_sum + spin(square_sum, half_row), cross_sum + spin(cross_sum, half_row))
    part_out[0] = part
    for slot, partner in enumerate(group_a):
        send(part_out.at[0], part_a.at[slot], 4, partner)

    shared = miss[8:] + pltpu.roll(miss_dot[8:], 4, 0)
    tiles = [miss[:8], miss_dot[:8], shared]
    for i, tile in enumerate(tiles):
        rim_out[i * 8 : i * 8 + 8] = tile
    rim_strip[...] = pack_strips(tiles)
    for dx, dy, _ in ALONG_X:
        send(rim_out, rim.at[pl.ds(RIM[-dx], RIM_ROWS)], 2, at(dx, dy))
    for dx, dy in ACROSS:
        send(rim_strip, rim_y.at[STRIP[-dx, -dy]], 3, at(dx, dy))

    for dx, column in ADJ_MAIN.items():
        select_table(adj, column, adj_parts, soil_m[dx])
    for dx, column in ADJ_EDGE.items():
        select_table(adj, column, adj_parts, soil_e[dx])

    received(part_a, 4)
    part = part + jnp.sum(part_a[...], 0)
    part_out[1] = part
    for slot, partner in enumerate(group_b):
        send(part_out.at[1], part_b.at[slot], 5, partner)

    received(rim, 2)
    received(rim_y, 3)
    lam_m, lam_e, mu_m, mu_e = {}, {}, {}, {}

    def rim_fields(tiles):
        fields = jnp.stack([tiles[0], tiles[2], tiles[1], pltpu.roll(tiles[2], 4, 0)])
        fields = fields.reshape(2, 2, 8, LANES)
        return fields[:1], fields[1:]

    for dx in range(-STEPS, STEPS + 1):
        own = [rim[pl.ds(RIM[dx] + i * 8, 8)] for i in range(3)] if dx else tiles
        lam_m[dx], mu_m[dx] = rim_fields(own)
        if abs(dx) < STEPS:
            left, right = rim_y[STRIP[dx, -1]], rim_y[STRIP[dx, 1]]
            lam_e[dx], mu_e[dx] = rim_fields([unpack_strip(left, right, i) for i in range(3)])

    sums = {}

    def into(key, value):
        value = value[:, 0] + value[:, 1]
        if key in sums:
            old = sums[key]
            n = old.shape[0]
            sums[key] = jnp.concatenate([old + value[:n], value[n:]], 0) if value.shape[0] > n else old + value
        else:
            sums[key] = value

    own = (("xm", 0), ("xm", -1), ("zm", 0), ("ym", 0), ("ye", 0))
    for k in reversed(range(STEPS)):
        reach = STEPS - 1 - k
        u_m = {dx: mixed(adj, ADJ_MAIN[dx], lam_m[dx]) for dx in lam_m}
        v_m = {dx: mixed(adj, ADJ_MAIN[dx], mu_m[dx]) for dx in mu_m}
        u_e = {dx: mixed(adj, ADJ_EDGE[dx], lam_e[dx]) for dx in lam_e}
        v_e = {dx: mixed(adj, ADJ_EDGE[dx], mu_e[dx]) for dx in mu_e}
        diff_u, diff_v = faces(u_m, u_e, True), faces(v_m, v_e, True)
        for key in own:
            du, dv, dc = diff_u[key], diff_v[key], diffs[k][key][: diff_u[key].shape[0]]
            into(("g", key), du * dc)
            second = dv * dc
            if diffs_dot[k] is not None:
                second = second + du * diffs_dot[k][key][: du.shape[0]]
            into(("h", key), second)
        if k == 0:
            break
        need = lambda diff: {
            key: value for key, value in diff.items()
            if key[0][0] == "x" or abs(key[1]) <= (k if key[0] != "ze" else k - 1)
        }
        diff_u, diff_v = need(diff_u), need(diff_v)
        step_m, step_e = gathered(times(coeff, diff_u), k, True)
        dot_m, dot_e = gathered(plus(times(coeff, diff_v), times(slope, diff_u)), k, True)

        def added(old, step):
            n = old.shape[0]
            return jnp.concatenate([old + step[:n], step[n:]], 0)

        lam_m, lam_e = (
            {dx: added(lam_m[dx], step_m[dx]) for dx in step_m},
            {dx: added(lam_e[dx], step_e[dx]) for dx in step_e},
        )
        mu_m, mu_e = (
            {dx: added(mu_m[dx], dot_m[dx]) for dx in dot_m},
            {dx: added(mu_e[dx], dot_e[dx]) for dx in dot_e},
        )

    def per_cell(name):
        y_sum = sums[name, ("ym", 0)]
        side = sums[name, ("xm", 0)] + sums[name, ("xm", -1)] + y_sum
        side = side + y_prev(y_sum, sums[name, ("ye", 0)])[0]
        depth = sums[name, ("zm", 0)]
        n = side.shape[0]
        total = jnp.concatenate([side + depth[:n] + depth[1:], depth[n:]], 0)
        return jnp.sum(total, 1, keepdims=True)

    weight = weight_m[0][:, 0, :1, :]
    plain_part = -weight * per_cell("g")
    dot_part = -weight * per_cell("h") + own_dire[:, 0, :1, :] * plain_part

    received(part_b, 5)
    part = part + jnp.sum(part_b[...], 0)
    total = jnp.sum(jnp.where(front, part, 0.0), 1, keepdims=True)
    cross = jnp.sum(jnp.where(front, 0.0, part), 1, keepdims=True)
    count = float(SPECIES * nx * ny * LANES)
    factor = count / total
    second = -2.0 * count * cross / (total * total)
    zero = jnp.zeros((1, LANES), jnp.float32)
    for z in range(16):
        one, two = (dot_part[z], plain_part[z]) if z <= STEPS else (zero, zero)
        out_ref[0, z : z + 1, :] = factor * one + second * two

    for number, buffer in enumerate((halo, halo_y, rim, rim_y, part_a, part_b)):
        sent(buffer, number)


def solution(mesh):
    nx, ny = mesh.shape["gx"], mesh.shape["gy"]

    def body(c_start, log_tort, direction, mix_inverse, pair_mask, soil_layer, observed):
        f32 = jnp.float32
        hbm = pl.BlockSpec(memory_space=pltpu.HBM)
        vmem = pl.BlockSpec(memory_space=pltpu.VMEM)
        return pl.pallas_call(
            lambda *refs: kernel(nx, ny, *refs),
            out_shape=jax.ShapeDtypeStruct((1, 16, LANES), f32),
            in_specs=[hbm] * 7,
            out_specs=vmem,
            scratch_shapes=[
                pltpu.VMEM((ROWS, 8, LANES), f32),
                pltpu.VMEM((1, LANES), jnp.int32),
                pltpu.VMEM((SPECIES, 1, LANES), f32),
                pltpu.VMEM((SPECIES, LAYERS, SPECIES), f32),
                pltpu.VMEM((SPECIES, SPECIES), jnp.int32),
                pltpu.VMEM(((STEPS + 1) * ROWS, LANES), f32),
                pltpu.VMEM((8, LANES), f32),
                pltpu.VMEM((HALO_ROWS, LANES), f32),
                pltpu.VMEM((len(ACROSS), 8, LANES), f32),
                pltpu.VMEM((RIM_ROWS, LANES), f32),
                pltpu.VMEM((8, LANES), f32),
                pltpu.VMEM((len(ALONG_X) * RIM_ROWS, LANES), f32),
                pltpu.VMEM((len(ACROSS), 8, LANES), f32),
                pltpu.VMEM((2, 1, LANES), f32),
                pltpu.VMEM((15, 1, LANES), f32),
                pltpu.VMEM((15, 1, LANES), f32),
                pltpu.VMEM((LANES, LANES), f32),
                pltpu.VMEM((LAYERS, SPECIES, 2, 8, LANES), f32),
                pltpu.VMEM((LAYERS, SPECIES, 2, 8, LANES), f32),
                pltpu.VMEM((8, SPECIES, 2, 8, LANES), f32),
                pltpu.VMEM((12, SPECIES, 2, 8, LANES), f32),
                pltpu.SemaphoreType.DMA((7,)),
                pltpu.SemaphoreType.DMA((6,)),
                pltpu.SemaphoreType.DMA((6,)),
            ],
            compiler_params=pltpu.CompilerParams(collective_id=0, has_side_effects=True),
        )(c_start, log_tort, direction, mix_inverse.transpose(1, 0, 2), pair_mask, soil_layer, observed)

    return jax.shard_map(
        body,
        mesh=mesh,
        in_specs=(
            P(None, "gx", None, "gy"),
            P("gx", None, "gy"),
            P("gx", None, "gy"),
            P(),
            P(),
            P("gx", "gy"),
            P(None, "gx", "gy"),
        ),
        out_specs=P("gx", None, "gy"),
        check_vma=False,
    )
```

```python
import jax
import jax.numpy as jnp
from jax import lax
from jax.experimental import pallas as pl
from jax.experimental.pallas import tpu as pltpu
from jax.sharding import PartitionSpec as P

MESH = pl.DeviceIdType.MESH
DT = 0.04
STEPS = 3
SPECIES = 12
LAYERS = 4
LANES = 128
ROWS = 16
TORT, DIRE, SOIL = 12, 13, 14
DIRECT = 1


def offsets():
    found = []
    for dx in range(-STEPS, STEPS + 1):
        for dy in (-1, 0, 1):
            depths = STEPS + 1 - abs(dx) - (1 if dy else 0)
            if depths > 0 and (dx or dy):
                found.append((dx, dy, depths))
    return found


ALONG_X = [(dx, dy, depths) for dx, dy, depths in offsets() if dy == 0]
ACROSS = [(dx, dy) for dx, dy, _ in offsets() if dy]
STRIP = {place: i for i, place in enumerate(ACROSS)}
SEM = {(dx, dy): i for i, (dx, dy, _) in enumerate(offsets())}
HALO, HALO_ROWS = {}, 0
for dx, _, depths in ALONG_X:
    HALO[dx] = HALO_ROWS
    HALO_ROWS += depths * ROWS
RIM_ROWS = 24
RIM = {dx: i * RIM_ROWS for i, (dx, _, _) in enumerate(ALONG_X)}
FWD_MAIN = {dx: i for i, dx in enumerate(range(-2, 3))}
FWD_EDGE = {dx: 5 + i for i, dx in enumerate(range(-1, 2))}
ADJ_MAIN = {dx: i for i, dx in enumerate(range(-3, 4))}
ADJ_EDGE = {dx: 7 + i for i, dx in enumerate(range(-2, 3))}


def lane(shape):
    return lax.broadcasted_iota(jnp.int32, shape, len(shape) - 1)


def spin(value, by):
    return pltpu.roll(value, by % LANES, value.ndim - 1)


def y_next(main, edge):
    last = lane(main.shape) == LANES - 1
    a, b = spin(main, -1), spin(edge, -1)
    return jnp.where(last, b, a), jnp.where(last, a, b)


def y_prev(main, edge):
    first = lane(main.shape) == 0
    a, b = spin(main, 1), spin(edge, 1)
    return jnp.where(first, b, a), jnp.where(first, a, b)


def pack_strips(tiles):
    group = lane((8, LANES)) // 8
    packed = tiles[0]
    for i, tile in enumerate(tiles[1:], 1):
        packed = jnp.where(group == i, spin(tile, 8 * i), packed)
        packed = jnp.where(group == 15 - i, spin(tile, -8 * i), packed)
    return packed


def unpack_strip(left, right, i):
    return jnp.where(lane((8, LANES)) < LANES // 2, spin(right, -8 * i), spin(left, 8 * i))


def faces(main, edge, closed):
    out = {}
    for kind, field in (("m", main), ("e", edge)):
        for dx in field:
            value = field[dx]
            if dx + 1 in field:
                n = min(value.shape[0], field[dx + 1].shape[0])
                out["x" + kind, dx] = field[dx + 1][:n] - value[:n]
            parts = [value[:1]]
            if value.shape[0] > 1:
                parts.append(value[1:] - value[:-1])
            if closed:
                parts.append(-value[-1:])
            out["z" + kind, dx] = jnp.concatenate(parts, 0) if len(parts) > 1 else parts[0]
    for dx in edge:
        n = edge[dx].shape[0]
        a, b = y_next(main[dx][:n], edge[dx][:n])
        out["ym", dx] = a - main[dx][:n]
        out["ye", dx] = b - edge[dx][:n]
    return out


def times(coeff, diff):
    return {key: coeff[key][: diff[key].shape[0]] * diff[key] for key in diff}


def plus(one, two):
    return {key: one[key] + two[key] for key in one}


def gathered(flux, reach, closed):
    result = []
    for kind, most in (("m", reach), ("e", reach - 1)):
        field = {}
        for dx in range(-most, most + 1):
            depth = flux["z" + kind, dx]
            n = depth.shape[0] - 1
            total = depth[1:] - depth[:-1]
            a, b = y_prev(flux["ym", dx], flux["ye", dx])
            back = a if kind == "m" else b
            side = (
                flux["x" + kind, dx][:n]
                - flux["x" + kind, dx - 1][:n]
                + flux["y" + kind, dx][:n]
                - back[:n]
            )
            if closed:
                total = jnp.concatenate([total[:n] + side, -depth[n:]], 0)
            else:
                total = total + side
            field[dx] = total
        result.append(field)
    return result


def mixed(table, column, value):
    total = None
    for t in range(SPECIES):
        part = table[column, t] * value[:, t // 8 : t // 8 + 1, t % 8 : t % 8 + 1, :]
        total = part if total is None else total + part
    return total


def select_table(table, column, parts, soil):
    masks = [soil == float(level) for level in range(LAYERS)]
    for t in range(SPECIES):
        for half in range(2):
            value = jnp.zeros((8, LANES), jnp.float32)
            for level in range(LAYERS):
                value = jnp.where(masks[level], parts[level, t, half], value)
            table[column, t, half] = value


def kernel(
    nx, ny, c_hbm, m_hbm, d_hbm, mix_hbm, pair_hbm, soil_hbm, obs_hbm, out_ref,
    stage, soil_v, obs_v, mix_ref, pair_ref, block, strip, halo, halo_y, rim_out, rim_strip, rim, rim_y,
    part_out, part_all, part_b, part_sum,
    square, fwd_parts, adj_parts, fwd, adj,
    local_sem, send_sem, recv_sem, ready,
):
    x, y = lax.axis_index("gx"), lax.axis_index("gy")
    x_hi, x_mid, x_core = x // 8, (x // 2) % 4, x % 2
    y_hi, y_lo = y // 4, y % 4

    in_x = {dx: jnp.logical_and(x + dx >= 0, x + dx < nx) for dx in range(-STEPS, STEPS + 1)}
    all_in_x = jnp.logical_and(x >= STEPS, x < nx - STEPS)

    def neighbours(act, rows=(-1, 1, 0)):
        for dy in rows:
            places = [place for place in offsets() if place[1] == dy]

            def row(places=places):
                @pl.when(all_in_x)
                def _():
                    for place in places:
                        act(*place)

                @pl.when(jnp.logical_not(all_in_x))
                def _():
                    for place in places:
                        pl.when(in_x[place[0]])(lambda place=place: act(*place))

            if dy:
                pl.when(y > 0 if dy < 0 else y < ny - 1)(row)
            else:
                row()

    def signal(semaphore, partner):
        pl.semaphore_signal(semaphore, inc=1, device_id=partner, device_id_type=MESH)

    loads = [
        pltpu.make_async_copy(c_hbm.at[:, 0, 0:8], stage.at[0:SPECIES], local_sem.at[0]),
        pltpu.make_async_copy(m_hbm.at[0, 0:8], stage.at[TORT], local_sem.at[1]),
        pltpu.make_async_copy(d_hbm.at[0, 0:8], stage.at[DIRE], local_sem.at[2]),
        pltpu.make_async_copy(soil_hbm, soil_v, local_sem.at[3]),
        pltpu.make_async_copy(mix_hbm, mix_ref, local_sem.at[4]),
        pltpu.make_async_copy(pair_hbm, pair_ref, local_sem.at[5]),
        pltpu.make_async_copy(obs_hbm, obs_v, local_sem.at[6]),
    ]
    rim[...] = jnp.zeros_like(rim)
    rim_y[...] = jnp.zeros_like(rim_y)
    barrier = pltpu.get_barrier_semaphore()
    neighbours(lambda dx, dy, _: signal(barrier, (x + dx, y + dy)))
    for copy in loads:
        copy.start()
    group_a = []
    for i in range(1, 16):
        core, mid, high = i % 2, (i // 2) % 4, i // 8
        group_a.append((x_hi * 8 + (x_mid + mid) % 4 * 2 + (x_core + core) % 2, (y_hi + high) % 2 * 4 + y_lo))
    group_b = []
    for i in range(1, 16):
        group_b.append(((x_hi + i // 4) % 4 * 8 + x_mid * 2 + x_core, y_hi * 4 + (y_lo + i % 4) % 4))
    direct = jnp.logical_and(y_hi == 0, x_mid < DIRECT)
    for partner in group_a + group_b:
        signal(barrier, partner)
    arrivals = len(group_a + group_b)
    for dx, dy, _ in offsets():
        there = in_x[dx]
        if dy:
            there = jnp.logical_and(there, y > 0 if dy < 0 else y < ny - 1)
        arrivals = arrivals + there.astype(jnp.int32)

    stage[SOIL] = jnp.zeros((8, LANES), jnp.float32)
    stage[SOIL + 1] = jnp.zeros((8, LANES), jnp.float32)
    for copy in loads[:4]:
        copy.wait()
    stage[SOIL, 0:1] = soil_v[...].astype(jnp.float32)
    flat = stage.reshape(ROWS * 8, LANES)
    for z in range(STEPS + 1):
        for half in range(2):
            block[pl.ds(z * ROWS + half * 8, 8)] = flat[pl.ds(half * 64 + z, 8, stride=8)]
    strip[...] = pack_strips([block[i * 8 : i * 8 + 8] for i in range(2 * STEPS)])

    pl.semaphore_wait(barrier, arrivals)

    @pl.when(direct)
    def _():
        for partner in group_a:
            signal(ready, partner)


    def copy_of(src, dst, sems, number, partner):
        return pltpu.make_async_remote_copy(
            src_ref=src, dst_ref=dst, send_sem=send_sem.at[sems + number], recv_sem=recv_sem.at[sems + number],
            device_id=partner, device_id_type=MESH,
        )

    def halo_copy(dx, dy, depths):
        if dy:
            src, dst = strip, halo_y.at[STRIP[-dx, -dy]]
        else:
            src, dst = block.at[pl.ds(0, depths * ROWS)], halo.at[pl.ds(HALO[-dx], depths * ROWS)]
        return copy_of(src, dst, 0, SEM[-dx, -dy], (x + dx, y + dy))

    def rim_copy(dx, dy, _):
        if dy:
            src, dst = rim_strip, rim_y.at[STRIP[-dx, -dy]]
        else:
            src, dst = rim_out, rim.at[pl.ds(RIM[-dx], RIM_ROWS)]
        return copy_of(src, dst, len(SEM), SEM[-dx, -dy], (x + dx, y + dy))

    def part_copy(index, dst, partner):
        return copy_of(part_out.at[index % 2], dst, 2 * len(SEM), index, partner)

    neighbours(lambda *place: halo_copy(*place).start())

    for copy in loads[4:]:
        copy.wait()
    square[...] = jnp.zeros((LANES, LANES), jnp.float32)
    diagonal = lax.broadcasted_iota(jnp.int32, (SPECIES, SPECIES), 0) == lax.broadcasted_iota(
        jnp.int32, (SPECIES, SPECIES), 1
    )
    pair = pair_ref[...].astype(jnp.float32)
    for level in range(LAYERS):
        entry = mix_ref[:, level, :]
        square[level * ROWS : level * ROWS + SPECIES, 0:SPECIES] = jnp.where(diagonal, entry, entry * pair)
    plain = square[...]
    turned = plain.T
    for level in range(LAYERS):
        for t in range(SPECIES):
            for half in range(2):
                row = level * ROWS + half * 8
                fwd_parts[level, t, half] = jnp.broadcast_to(plain[row : row + 8, t : t + 1], (8, LANES))
                col = level * ROWS + t
                adj_parts[level, t, half] = jnp.broadcast_to(
                    turned[half * 8 : half * 8 + 8, col : col + 1], (8, LANES)
                )

    def arrived(copy, rows=(-1, 1, 0)):
        def act(dx, dy, depths):
            copy(-dx, -dy, depths).wait_recv()
        neighbours(act, rows)

    species_row = lax.broadcasted_iota(jnp.int32, (1, 2, 8, LANES), 1) * 8 + lax.broadcasted_iota(
        jnp.int32, (1, 2, 8, LANES), 2
    )
    right_half = lane((8, LANES)) < LANES // 2
    in_y = jnp.where(right_half, y + 1, y - 1)
    in_y = jnp.logical_and(in_y >= 0, in_y < ny)

    def cells(ref, start, depths):
        return ref[pl.ds(start, depths * ROWS)].reshape(depths, 2, 8, LANES)

    def row_of(value, row):
        depths = value.shape[0]
        return jnp.broadcast_to(value[:, row // 8, row % 8 : row % 8 + 1, :], (depths, 8, LANES))

    def zero_unless(valid, value):
        return jnp.where(jnp.broadcast_to(valid, value.shape), value, 0.0)

    def unpack(value, valid):
        depths = value.shape[0]
        state = jnp.where(jnp.broadcast_to(species_row < SPECIES, value.shape), value, 0.0)
        tort, dire = row_of(value, TORT), row_of(value, DIRE)
        soil = row_of(value[:1], SOIL)[0]
        if valid is not None:
            state = zero_unless(valid, state)
            tort, dire = zero_unless(valid, tort), zero_unless(valid, dire)
            soil = jnp.where(valid, soil, -1.0)
        weight = (0.5 * DT) * jnp.exp(tort)
        turn = weight * dire
        shape = (depths, 1, 8, LANES)
        return state, weight.reshape(shape), turn.reshape(shape), dire.reshape(shape), soil

    main, edge = {}, {}
    weight_m, weight_e, turn_m, turn_e, soil_m, soil_e = {}, {}, {}, {}, {}, {}
    main[0], weight_m[0], turn_m[0], own_dire, soil_m[0] = unpack(cells(block, 0, STEPS + 1), None)
    select_table(fwd, FWD_MAIN[0], fwd_parts, soil_m[0])

    arrived(halo_copy, (-1, 1))
    for dx in range(1 - STEPS, STEPS):
        depths = STEPS - abs(dx)
        left, right = halo_y[STRIP[dx, -1]], halo_y[STRIP[dx, 1]]
        raw = jnp.stack([unpack_strip(left, right, i) for i in range(2 * depths)])
        valid = jnp.logical_and(in_y, jnp.broadcast_to(in_x[dx], (8, LANES)))
        edge[dx], weight_e[dx], turn_e[dx], _, soil_e[dx] = unpack(raw.reshape(depths, 2, 8, LANES), valid)
    for dx, column in FWD_EDGE.items():
        select_table(fwd, column, fwd_parts, soil_e[dx])

    arrived(halo_copy, (0,))
    for dx, _, depths in ALONG_X:
        valid = jnp.broadcast_to(in_x[dx], (8, LANES))
        main[dx], weight_m[dx], turn_m[dx], _, soil_m[dx] = unpack(cells(halo, HALO[dx], depths), valid)
    main, weight_m, turn_m = ({dx: field[dx] for dx in sorted(field)} for field in (main, weight_m, turn_m))
    for dx, column in FWD_MAIN.items():
        if dx:
            select_table(fwd, column, fwd_parts, soil_m[dx])

    def face_sums(main_w, edge_w, outside):
        out = {}
        for kind, field in (("m", main_w), ("e", edge_w)):
            for dx in field:
                value = field[dx]
                if dx + 1 in field:
                    n = min(value.shape[0], field[dx + 1].shape[0])
                    out["x" + kind, dx] = field[dx + 1][:n] + value[:n]
                parts = [value[:1] + outside]
                if value.shape[0] > 1:
                    parts.append(value[1:] + value[:-1])
                out["z" + kind, dx] = jnp.concatenate(parts, 0) if len(parts) > 1 else parts[0]
        for dx in edge_w:
            n = edge_w[dx].shape[0]
            a, b = y_next(main_w[dx][:n], edge_w[dx][:n])
            out["ym", dx] = a + main_w[dx][:n]
            out["ye", dx] = b + edge_w[dx][:n]
        return out

    coeff = face_sums(weight_m, weight_e, 0.5 * DT)
    slope = face_sums(turn_m, turn_e, 0.0)

    diffs, diffs_dot = [], []
    main_dot, edge_dot = None, None
    for k in range(STEPS):
        reach = STEPS - 1 - k
        diff = faces(main, edge, False)
        diffs.append(diff)
        flux = times(coeff, diff)
        flux_dot = times(slope, diff)
        if main_dot is not None:
            diff_dot = faces(main_dot, edge_dot, False)
            flux_dot = plus(flux_dot, times(coeff, diff_dot))
        else:
            diff_dot = None
        diffs_dot.append(diff_dot)
        spread_m, spread_e = gathered(flux, reach, False)
        dot_m, dot_e = gathered(flux_dot, reach, False)
        new = [{}, {}, {}, {}]
        for kind, table, old, old_dot, spread, dot in (
            (0, FWD_MAIN, main, main_dot, spread_m, dot_m),
            (1, FWD_EDGE, edge, edge_dot, spread_e, dot_e),
        ):
            for dx in spread:
                n = spread[dx].shape[0]
                new[kind][dx] = old[dx][:n] + mixed(fwd, table[dx], spread[dx])
                moved = mixed(fwd, table[dx], dot[dx])
                new[2 + kind][dx] = moved if old_dot is None else old_dot[dx][:n] + moved
        main, edge, main_dot, edge_dot = new

    obs = jnp.concatenate([obs_v[s] for s in range(SPECIES)] + [jnp.zeros((ROWS - SPECIES, LANES), jnp.float32)], 0)
    miss = main[0].reshape(ROWS, LANES) - obs
    miss_dot = main_dot[0].reshape(ROWS, LANES)
    square_sum = jnp.sum(miss * miss, 0, keepdims=True)
    cross_sum = jnp.sum(miss * miss_dot, 0, keepdims=True)
    front = lane((1, LANES)) < LANES // 2
    half_row = LANES // 2
    part = jnp.where(front, square_sum + spin(square_sum, half_row), cross_sum + spin(cross_sum, half_row))
    part_out[0] = part
    for slot, partner in enumerate(group_a):
        part_copy(0, part_all.at[slot], partner).start()
    pl.semaphore_wait(ready, 2 * DIRECT - direct.astype(jnp.int32))
    for mid in range(DIRECT):
        for core in range(2):
            step = (core + x_core) % 2 + (mid - x_mid + 4) % 4 * 2 + y_hi * 8
            for i in range(1, 16):
                partner = (x_hi + i // 4) % 4 * 8 + mid * 2 + core, (y_lo + i % 4) % 4
                part_copy(2, part_all.at[i * 16 - 1 + step], partner).start()

    shared = miss[8:] + pltpu.roll(miss_dot[8:], 4, 0)
    tiles = [miss[:8], miss_dot[:8], shared]
    for i, tile in enumerate(tiles):
        rim_out[i * 8 : i * 8 + 8] = tile
    rim_strip[...] = pack_strips(tiles)
    neighbours(lambda *place: rim_copy(*place).start())

    for dx, column in ADJ_MAIN.items():
        select_table(adj, column, adj_parts, soil_m[dx])
    for dx, column in ADJ_EDGE.items():
        select_table(adj, column, adj_parts, soil_e[dx])

    near, far = part_all.at[pl.ds(0, 15)], part_all.at[pl.ds(15, 240)]

    def all_arrived(buffer, index):
        pltpu.make_async_copy(buffer, buffer, recv_sem.at[2 * len(SEM) + index]).wait()

    @pl.when(jnp.logical_not(direct))
    def _():
        all_arrived(near, 0)
        part_out[1] = part + jnp.sum(part_all[0:15], 0)
        for slot, partner in enumerate(group_b):
            part_copy(1, part_b.at[slot], partner).start()

    arrived(rim_copy)
    lam_m, lam_e, mu_m, mu_e = {}, {}, {}, {}

    def rim_fields(tiles):
        fields = jnp.stack([tiles[0], tiles[2], tiles[1], pltpu.roll(tiles[2], 4, 0)])
        fields = fields.reshape(2, 2, 8, LANES)
        return fields[:1], fields[1:]

    for dx in range(-STEPS, STEPS + 1):
        own = [rim[pl.ds(RIM[dx] + i * 8, 8)] for i in range(3)] if dx else tiles
        lam_m[dx], mu_m[dx] = rim_fields(own)
        if abs(dx) < STEPS:
            left, right = rim_y[STRIP[dx, -1]], rim_y[STRIP[dx, 1]]
            lam_e[dx], mu_e[dx] = rim_fields([unpack_strip(left, right, i) for i in range(3)])

    sums = {}

    def into(key, value):
        value = value[:, 0] + value[:, 1]
        if key in sums:
            old = sums[key]
            n = old.shape[0]
            sums[key] = jnp.concatenate([old + value[:n], value[n:]], 0) if value.shape[0] > n else old + value
        else:
            sums[key] = value

    own = (("xm", 0), ("xm", -1), ("zm", 0), ("ym", 0), ("ye", 0))
    for k in reversed(range(STEPS)):
        reach = STEPS - 1 - k
        u_m = {dx: mixed(adj, ADJ_MAIN[dx], lam_m[dx]) for dx in lam_m}
        v_m = {dx: mixed(adj, ADJ_MAIN[dx], mu_m[dx]) for dx in mu_m}
        u_e = {dx: mixed(adj, ADJ_EDGE[dx], lam_e[dx]) for dx in lam_e}
        v_e = {dx: mixed(adj, ADJ_EDGE[dx], mu_e[dx]) for dx in mu_e}
        diff_u, diff_v = faces(u_m, u_e, True), faces(v_m, v_e, True)
        for key in own:
            du, dv, dc = diff_u[key], diff_v[key], diffs[k][key][: diff_u[key].shape[0]]
            into(("g", key), du * dc)
            second = dv * dc
            if diffs_dot[k] is not None:
                second = second + du * diffs_dot[k][key][: du.shape[0]]
            into(("h", key), second)
        if k == 0:
            break
        need = lambda diff: {
            key: value for key, value in diff.items()
            if key[0][0] == "x" or abs(key[1]) <= (k if key[0] != "ze" else k - 1)
        }
        diff_u, diff_v = need(diff_u), need(diff_v)
        step_m, step_e = gathered(times(coeff, diff_u), k, True)
        dot_m, dot_e = gathered(plus(times(coeff, diff_v), times(slope, diff_u)), k, True)

        def added(old, step):
            n = old.shape[0]
            return jnp.concatenate([old + step[:n], step[n:]], 0)

        lam_m, lam_e = (
            {dx: added(lam_m[dx], step_m[dx]) for dx in step_m},
            {dx: added(lam_e[dx], step_e[dx]) for dx in step_e},
        )
        mu_m, mu_e = (
            {dx: added(mu_m[dx], dot_m[dx]) for dx in dot_m},
            {dx: added(mu_e[dx], dot_e[dx]) for dx in dot_e},
        )

    def per_cell(name):
        y_sum = sums[name, ("ym", 0)]
        side = sums[name, ("xm", 0)] + sums[name, ("xm", -1)] + y_sum
        side = side + y_prev(y_sum, sums[name, ("ye", 0)])[0]
        depth = sums[name, ("zm", 0)]
        n = side.shape[0]
        total = jnp.concatenate([side + depth[:n] + depth[1:], depth[n:]], 0)
        return jnp.sum(total, 1, keepdims=True)

    weight = weight_m[0][:, 0, :1, :]
    plain_part = -weight * per_cell("g")
    dot_part = -weight * per_cell("h") + own_dire[:, 0, :1, :] * plain_part

    neighbours(lambda *place: halo_copy(*place).wait_send())
    neighbours(lambda *place: rim_copy(*place).wait_send())
    def all_sent(buffer, index):
        pltpu.make_async_copy(buffer, buffer, send_sem.at[2 * len(SEM) + index]).wait()

    all_sent(near, 0)
    all_sent(part_all.at[pl.ds(0, 30 * DIRECT)], 2)

    @pl.when(direct)
    def _():
        all_arrived(near, 0)
        all_arrived(far, 2)
        rest = part_all[...].reshape(17, 15, 1, LANES)
        part_sum[...] = part_out[0] + jnp.sum(jnp.sum(rest, 0), 0)

    @pl.when(jnp.logical_not(direct))
    def _():
        all_sent(part_b, 1)
        all_arrived(part_b, 1)
        part_sum[...] = part_out[1] + jnp.sum(part_b[...], 0)

    part = part_sum[...]
    total = jnp.sum(jnp.where(front, part, 0.0), 1, keepdims=True)
    cross = jnp.sum(jnp.where(front, 0.0, part), 1, keepdims=True)
    count = float(SPECIES * nx * ny * LANES)
    factor = count / total
    second = -2.0 * count * cross / (total * total)
    zero = jnp.zeros((1, LANES), jnp.float32)
    for z in range(16):
        one, two = (dot_part[z], plain_part[z]) if z <= STEPS else (zero, zero)
        out_ref[0, z : z + 1, :] = factor * one + second * two


def solution(mesh):
    nx, ny = mesh.shape["gx"], mesh.shape["gy"]

    def body(c_start, log_tort, direction, mix_inverse, pair_mask, soil_layer, observed):
        f32 = jnp.float32
        hbm = pl.BlockSpec(memory_space=pltpu.HBM)
        vmem = pl.BlockSpec(memory_space=pltpu.VMEM)
        return pl.pallas_call(
            lambda *refs: kernel(nx, ny, *refs),
            out_shape=jax.ShapeDtypeStruct((1, 16, LANES), f32),
            in_specs=[hbm] * 7,
            out_specs=vmem,
            scratch_shapes=[
                pltpu.VMEM((ROWS, 8, LANES), f32),
                pltpu.VMEM((1, LANES), jnp.int32),
                pltpu.VMEM((SPECIES, 1, LANES), f32),
                pltpu.VMEM((SPECIES, LAYERS, SPECIES), f32),
                pltpu.VMEM((SPECIES, SPECIES), jnp.int32),
                pltpu.VMEM(((STEPS + 1) * ROWS, LANES), f32),
                pltpu.VMEM((8, LANES), f32),
                pltpu.VMEM((HALO_ROWS, LANES), f32),
                pltpu.VMEM((len(ACROSS), 8, LANES), f32),
                pltpu.VMEM((RIM_ROWS, LANES), f32),
                pltpu.VMEM((8, LANES), f32),
                pltpu.VMEM((len(ALONG_X) * RIM_ROWS, LANES), f32),
                pltpu.VMEM((len(ACROSS), 8, LANES), f32),
                pltpu.VMEM((2, 1, LANES), f32),
                pltpu.VMEM((255, 1, LANES), f32),
                pltpu.VMEM((15, 1, LANES), f32),
                pltpu.VMEM((1, LANES), f32),
                pltpu.VMEM((LANES, LANES), f32),
                pltpu.VMEM((LAYERS, SPECIES, 2, 8, LANES), f32),
                pltpu.VMEM((LAYERS, SPECIES, 2, 8, LANES), f32),
                pltpu.VMEM((8, SPECIES, 2, 8, LANES), f32),
                pltpu.VMEM((12, SPECIES, 2, 8, LANES), f32),
                pltpu.SemaphoreType.DMA((7,)),
                pltpu.SemaphoreType.DMA((2 * len(SEM) + 3,)),
                pltpu.SemaphoreType.DMA((2 * len(SEM) + 3,)),
                pltpu.SemaphoreType.REGULAR,
            ],
            compiler_params=pltpu.CompilerParams(
                collective_id=0, has_side_effects=True, vmem_limit_bytes=32 * 1024 * 1024
            ),
        )(*(
            pltpu.with_memory_space_constraint(value, pltpu.HBM)
            for value in (
                c_start, log_tort, direction, mix_inverse.transpose(1, 0, 2), pair_mask, soil_layer, observed,
            )
        ))

    return jax.shard_map(
        body,
        mesh=mesh,
        in_specs=(
            P(None, "gx", None, "gy"),
            P("gx", None, "gy"),
            P("gx", None, "gy"),
            P(),
            P(),
            P("gx", "gy"),
            P(None, "gx", "gy"),
        ),
        out_specs=P("gx", None, "gy"),
        check_vma=False,
    )
```

```python
import jax
import jax.numpy as jnp
from jax import lax
from jax.experimental import pallas as pl
from jax.experimental.pallas import tpu as pltpu
from jax.sharding import PartitionSpec as P

MESH = pl.DeviceIdType.MESH
DT = 0.04
STEPS = 3
SPECIES = 12
LAYERS = 4
LANES = 128
ROWS = 16
TORT, DIRE, SOIL = 12, 13, 14


def offsets():
    found = []
    for dx in range(-STEPS, STEPS + 1):
        for dy in (-1, 0, 1):
            depths = STEPS + 1 - abs(dx) - (1 if dy else 0)
            if depths > 0 and (dx or dy):
                found.append((dx, dy, depths))
    return found


ALONG_X = [(dx, dy, depths) for dx, dy, depths in offsets() if dy == 0]
ACROSS = [(dx, dy) for dx, dy, _ in offsets() if dy]
STRIP = {place: i for i, place in enumerate(ACROSS)}
SEM = {(dx, dy): i for i, (dx, dy, _) in enumerate(offsets())}
HALO, HALO_ROWS = {}, 0
for dx, _, depths in ALONG_X:
    HALO[dx] = HALO_ROWS
    HALO_ROWS += depths * ROWS
RIM_ROWS = 24
RIM = {dx: i * RIM_ROWS for i, (dx, _, _) in enumerate(ALONG_X)}
FWD_MAIN = {dx: i for i, dx in enumerate(range(-2, 3))}
FWD_EDGE = {dx: 5 + i for i, dx in enumerate(range(-1, 2))}
ADJ_MAIN = {dx: i for i, dx in enumerate(range(-3, 4))}
ADJ_EDGE = {dx: 7 + i for i, dx in enumerate(range(-2, 3))}


def lane(shape):
    return lax.broadcasted_iota(jnp.int32, shape, len(shape) - 1)


def spin(value, by):
    return pltpu.roll(value, by % LANES, value.ndim - 1)


def y_next(main, edge):
    last = lane(main.shape) == LANES - 1
    a, b = spin(main, -1), spin(edge, -1)
    return jnp.where(last, b, a), jnp.where(last, a, b)


def y_prev(main, edge):
    first = lane(main.shape) == 0
    a, b = spin(main, 1), spin(edge, 1)
    return jnp.where(first, b, a), jnp.where(first, a, b)


def pack_strips(tiles):
    group = lane((8, LANES)) // 8
    packed = tiles[0]
    for i, tile in enumerate(tiles[1:], 1):
        packed = jnp.where(group == i, spin(tile, 8 * i), packed)
        packed = jnp.where(group == 15 - i, spin(tile, -8 * i), packed)
    return packed


FOLD = 48


def fold_strips(packed):
    place = lane((8, LANES))
    last = jnp.where(place >= LANES - FOLD, packed, pltpu.roll(spin(packed, -FOLD), 4, 0))
    first = jnp.where(place < FOLD, packed, pltpu.roll(spin(packed, FOLD), 4, 0))
    return last[:4], first[:4]


def unfold_strips(left, right):
    return jnp.concatenate([left, spin(left, FOLD)], 0), jnp.concatenate([right, spin(right, -FOLD)], 0)


def unpack_strip(left, right, i):
    return jnp.where(lane((8, LANES)) < LANES // 2, spin(right, -8 * i), spin(left, 8 * i))


def faces(main, edge, closed):
    out = {}
    for kind, field in (("m", main), ("e", edge)):
        for dx in field:
            value = field[dx]
            if dx + 1 in field:
                n = min(value.shape[0], field[dx + 1].shape[0])
                out["x" + kind, dx] = field[dx + 1][:n] - value[:n]
            parts = [value[:1]]
            if value.shape[0] > 1:
                parts.append(value[1:] - value[:-1])
            if closed:
                parts.append(-value[-1:])
            out["z" + kind, dx] = jnp.concatenate(parts, 0) if len(parts) > 1 else parts[0]
    for dx in edge:
        n = edge[dx].shape[0]
        a, b = y_next(main[dx][:n], edge[dx][:n])
        out["ym", dx] = a - main[dx][:n]
        out["ye", dx] = b - edge[dx][:n]
    return out


def times(coeff, diff):
    return {key: coeff[key][: diff[key].shape[0]] * diff[key] for key in diff}


def plus(one, two):
    return {key: one[key] + two[key] for key in one}


def gathered(flux, reach, closed):
    result = []
    for kind, most in (("m", reach), ("e", reach - 1)):
        field = {}
        for dx in range(-most, most + 1):
            depth = flux["z" + kind, dx]
            n = depth.shape[0] - 1
            total = depth[1:] - depth[:-1]
            a, b = y_prev(flux["ym", dx], flux["ye", dx])
            back = a if kind == "m" else b
            side = (
                flux["x" + kind, dx][:n]
                - flux["x" + kind, dx - 1][:n]
                + flux["y" + kind, dx][:n]
                - back[:n]
            )
            if closed:
                total = jnp.concatenate([total[:n] + side, -depth[n:]], 0)
            else:
                total = total + side
            field[dx] = total
        result.append(field)
    return result


def mixed(table, column, value):
    total = None
    for t in range(SPECIES):
        part = table[column, t] * value[:, t // 8 : t // 8 + 1, t % 8 : t % 8 + 1, :]
        total = part if total is None else total + part
    return total


def select_table(table, column, parts, soil):
    masks = [soil == float(level) for level in range(LAYERS)]
    for t in range(SPECIES):
        for half in range(2):
            value = jnp.zeros((8, LANES), jnp.float32)
            for level in range(LAYERS):
                value = jnp.where(masks[level], parts[level, t, half], value)
            table[column, t, half] = value


def kernel(
    nx, ny, c_hbm, m_hbm, d_hbm, mix_hbm, pair_hbm, soil_hbm, obs_hbm, out_ref,
    stage, soil_v, obs_v, mix_ref, pair_ref, block, strip, halo, halo_y, rim_out, rim_strip, rim, rim_y,
    part_out, part_all, part_b, part_sum,
    square, fwd_parts, adj_parts, fwd, adj,
    local_sem, send_sem, recv_sem, ready,
):
    x, y = lax.axis_index("gx"), lax.axis_index("gy")
    x_hi, x_mid, x_core = x // 8, (x // 2) % 4, x % 2
    y_hi, y_lo = y // 4, y % 4

    in_x = {dx: jnp.logical_and(x + dx >= 0, x + dx < nx) for dx in range(-STEPS, STEPS + 1)}
    all_in_x = jnp.logical_and(x >= STEPS, x < nx - STEPS)

    def neighbours(act, rows=(-1, 1, 0)):
        for dy in rows:
            places = [place for place in offsets() if place[1] == dy]

            def row(places=places):
                @pl.when(all_in_x)
                def _():
                    for place in places:
                        act(*place)

                @pl.when(jnp.logical_not(all_in_x))
                def _():
                    for place in places:
                        pl.when(in_x[place[0]])(lambda place=place: act(*place))

            if dy:
                pl.when(y > 0 if dy < 0 else y < ny - 1)(row)
            else:
                row()

    def signal(semaphore, partner):
        pl.semaphore_signal(semaphore, inc=1, device_id=partner, device_id_type=MESH)

    loads = [
        pltpu.make_async_copy(c_hbm.at[:, 0, 0:8], stage.at[0:SPECIES], local_sem.at[0]),
        pltpu.make_async_copy(m_hbm.at[0, 0:8], stage.at[TORT], local_sem.at[1]),
        pltpu.make_async_copy(d_hbm.at[0, 0:8], stage.at[DIRE], local_sem.at[2]),
        pltpu.make_async_copy(soil_hbm, soil_v, local_sem.at[3]),
        pltpu.make_async_copy(mix_hbm, mix_ref, local_sem.at[4]),
        pltpu.make_async_copy(pair_hbm, pair_ref, local_sem.at[5]),
        pltpu.make_async_copy(obs_hbm, obs_v, local_sem.at[6]),
    ]
    rim[...] = jnp.zeros_like(rim)
    rim_y[...] = jnp.zeros_like(rim_y)
    barrier = pltpu.get_barrier_semaphore()
    neighbours(lambda dx, dy, _: signal(barrier, (x + dx, y + dy)))
    for copy in loads:
        copy.start()
    group_a = []
    for i in range(1, 16):
        core, mid, high = i % 2, (i // 2) % 4, i // 8
        group_a.append((x_hi * 8 + (x_mid + mid) % 4 * 2 + (x_core + core) % 2, (y_hi + high) % 2 * 4 + y_lo))
    group_b = []
    for i in range(1, 16):
        group_b.append(((x_hi + i // 4) % 4 * 8 + x_mid * 2 + x_core, y_hi * 4 + (y_lo + i % 4) % 4))
    direct = jnp.logical_and(y_hi == 0, x_mid < 2)
    for partner in group_a + group_b:
        signal(barrier, partner)
    arrivals = len(group_a + group_b)
    for dx, dy, _ in offsets():
        there = in_x[dx]
        if dy:
            there = jnp.logical_and(there, y > 0 if dy < 0 else y < ny - 1)
        arrivals = arrivals + there.astype(jnp.int32)

    stage[SOIL] = jnp.zeros((8, LANES), jnp.float32)
    stage[SOIL + 1] = jnp.zeros((8, LANES), jnp.float32)
    for copy in loads[:4]:
        copy.wait()
    stage[SOIL, 0:1] = soil_v[...].astype(jnp.float32)
    flat = stage.reshape(ROWS * 8, LANES)
    for z in range(STEPS + 1):
        for half in range(2):
            block[pl.ds(z * ROWS + half * 8, 8)] = flat[pl.ds(half * 64 + z, 8, stride=8)]
    strip[0], strip[1] = fold_strips(pack_strips([block[i * 8 : i * 8 + 8] for i in range(2 * STEPS)]))

    pl.semaphore_wait(barrier, arrivals)

    @pl.when(direct)
    def _():
        for partner in group_a:
            signal(ready, partner)


    def copy_of(src, dst, sems, number, partner):
        return pltpu.make_async_remote_copy(
            src_ref=src, dst_ref=dst, send_sem=send_sem.at[sems + number], recv_sem=recv_sem.at[sems + number],
            device_id=partner, device_id_type=MESH,
        )

    def halo_copy(dx, dy, depths):
        if dy:
            src, dst = strip.at[(1 - dy) // 2], halo_y.at[STRIP[-dx, -dy]]
        else:
            src, dst = block.at[pl.ds(0, depths * ROWS)], halo.at[pl.ds(HALO[-dx], depths * ROWS)]
        return copy_of(src, dst, 0, SEM[-dx, -dy], (x + dx, y + dy))

    def rim_copy(dx, dy, _):
        if dy:
            src, dst = rim_strip.at[(1 - dy) // 2], rim_y.at[STRIP[-dx, -dy]]
        else:
            src, dst = rim_out, rim.at[pl.ds(RIM[-dx], RIM_ROWS)]
        return copy_of(src, dst, len(SEM), SEM[-dx, -dy], (x + dx, y + dy))

    def part_copy(index, dst, partner):
        return copy_of(part_out.at[index % 2], dst, 2 * len(SEM), index, partner)

    neighbours(lambda *place: halo_copy(*place).start(), (-1, 1))

    def along(places):
        @pl.when(all_in_x)
        def _():
            for place in places:
                halo_copy(*place).start()

        @pl.when(jnp.logical_not(all_in_x))
        def _():
            for place in places:
                pl.when(in_x[place[0]])(lambda place=place: halo_copy(*place).start())

    pl.when(x % 8 < 4)(lambda: along(ALONG_X))
    pl.when(x % 8 >= 4)(lambda: along(ALONG_X[::-1]))

    for copy in loads[4:]:
        copy.wait()
    square[...] = jnp.zeros((LANES, LANES), jnp.float32)
    diagonal = lax.broadcasted_iota(jnp.int32, (SPECIES, SPECIES), 0) == lax.broadcasted_iota(
        jnp.int32, (SPECIES, SPECIES), 1
    )
    pair = pair_ref[...].astype(jnp.float32)
    for level in range(LAYERS):
        entry = mix_ref[:, level, :]
        square[level * ROWS : level * ROWS + SPECIES, 0:SPECIES] = jnp.where(diagonal, entry, entry * pair)
    plain = square[...]
    turned = plain.T
    for level in range(LAYERS):
        for t in range(SPECIES):
            for half in range(2):
                row = level * ROWS + half * 8
                fwd_parts[level, t, half] = jnp.broadcast_to(plain[row : row + 8, t : t + 1], (8, LANES))
                col = level * ROWS + t
                adj_parts[level, t, half] = jnp.broadcast_to(
                    turned[half * 8 : half * 8 + 8, col : col + 1], (8, LANES)
                )

    def arrived(copy, rows=(-1, 1, 0)):
        def act(dx, dy, depths):
            copy(-dx, -dy, depths).wait_recv()
        neighbours(act, rows)

    species_row = lax.broadcasted_iota(jnp.int32, (1, 2, 8, LANES), 1) * 8 + lax.broadcasted_iota(
        jnp.int32, (1, 2, 8, LANES), 2
    )
    right_half = lane((8, LANES)) < LANES // 2
    in_y = jnp.where(right_half, y + 1, y - 1)
    in_y = jnp.logical_and(in_y >= 0, in_y < ny)

    def cells(ref, start, depths):
        return ref[pl.ds(start, depths * ROWS)].reshape(depths, 2, 8, LANES)

    def row_of(value, row):
        depths = value.shape[0]
        return jnp.broadcast_to(value[:, row // 8, row % 8 : row % 8 + 1, :], (depths, 8, LANES))

    def zero_unless(valid, value):
        return jnp.where(jnp.broadcast_to(valid, value.shape), value, 0.0)

    def unpack(value, valid):
        depths = value.shape[0]
        state = jnp.where(jnp.broadcast_to(species_row < SPECIES, value.shape), value, 0.0)
        tort, dire = row_of(value, TORT), row_of(value, DIRE)
        soil = row_of(value[:1], SOIL)[0]
        if valid is not None:
            state = zero_unless(valid, state)
            tort, dire = zero_unless(valid, tort), zero_unless(valid, dire)
            soil = jnp.where(valid, soil, -1.0)
        weight = (0.5 * DT) * jnp.exp(tort)
        turn = weight * dire
        shape = (depths, 1, 8, LANES)
        return state, weight.reshape(shape), turn.reshape(shape), dire.reshape(shape), soil

    main, edge = {}, {}
    weight_m, weight_e, turn_m, turn_e, soil_m, soil_e = {}, {}, {}, {}, {}, {}
    main[0], weight_m[0], turn_m[0], own_dire, soil_m[0] = unpack(cells(block, 0, STEPS + 1), None)
    select_table(fwd, FWD_MAIN[0], fwd_parts, soil_m[0])

    arrived(halo_copy, (-1, 1))
    for dx in range(1 - STEPS, STEPS):
        depths = STEPS - abs(dx)
        left, right = unfold_strips(halo_y[STRIP[dx, -1]], halo_y[STRIP[dx, 1]])
        raw = jnp.stack([unpack_strip(left, right, i) for i in range(2 * depths)])
        valid = jnp.logical_and(in_y, jnp.broadcast_to(in_x[dx], (8, LANES)))
        edge[dx], weight_e[dx], turn_e[dx], _, soil_e[dx] = unpack(raw.reshape(depths, 2, 8, LANES), valid)
    for dx, column in FWD_EDGE.items():
        select_table(fwd, column, fwd_parts, soil_e[dx])

    arrived(halo_copy, (0,))
    for dx, _, depths in ALONG_X:
        valid = jnp.broadcast_to(in_x[dx], (8, LANES))
        main[dx], weight_m[dx], turn_m[dx], _, soil_m[dx] = unpack(cells(halo, HALO[dx], depths), valid)
    main, weight_m, turn_m = ({dx: field[dx] for dx in sorted(field)} for field in (main, weight_m, turn_m))
    for dx, column in FWD_MAIN.items():
        if dx:
            select_table(fwd, column, fwd_parts, soil_m[dx])

    def face_sums(main_w, edge_w, outside):
        out = {}
        for kind, field in (("m", main_w), ("e", edge_w)):
            for dx in field:
                value = field[dx]
                if dx + 1 in field:
                    n = min(value.shape[0], field[dx + 1].shape[0])
                    out["x" + kind, dx] = field[dx + 1][:n] + value[:n]
                parts = [value[:1] + outside]
                if value.shape[0] > 1:
                    parts.append(value[1:] + value[:-1])
                out["z" + kind, dx] = jnp.concatenate(parts, 0) if len(parts) > 1 else parts[0]
        for dx in edge_w:
            n = edge_w[dx].shape[0]
            a, b = y_next(main_w[dx][:n], edge_w[dx][:n])
            out["ym", dx] = a + main_w[dx][:n]
            out["ye", dx] = b + edge_w[dx][:n]
        return out

    coeff = face_sums(weight_m, weight_e, 0.5 * DT)
    slope = face_sums(turn_m, turn_e, 0.0)

    diffs, diffs_dot = [], []
    main_dot, edge_dot = None, None
    for k in range(STEPS):
        reach = STEPS - 1 - k
        diff = faces(main, edge, False)
        diffs.append(diff)
        flux = times(coeff, diff)
        flux_dot = times(slope, diff)
        if main_dot is not None:
            diff_dot = faces(main_dot, edge_dot, False)
            flux_dot = plus(flux_dot, times(coeff, diff_dot))
        else:
            diff_dot = None
        diffs_dot.append(diff_dot)
        spread_m, spread_e = gathered(flux, reach, False)
        dot_m, dot_e = gathered(flux_dot, reach, False)
        new = [{}, {}, {}, {}]
        for kind, table, old, old_dot, spread, dot in (
            (0, FWD_MAIN, main, main_dot, spread_m, dot_m),
            (1, FWD_EDGE, edge, edge_dot, spread_e, dot_e),
        ):
            for dx in spread:
                n = spread[dx].shape[0]
                new[kind][dx] = old[dx][:n] + mixed(fwd, table[dx], spread[dx])
                moved = mixed(fwd, table[dx], dot[dx])
                new[2 + kind][dx] = moved if old_dot is None else old_dot[dx][:n] + moved
        main, edge, main_dot, edge_dot = new

    obs = jnp.concatenate([obs_v[s] for s in range(SPECIES)] + [jnp.zeros((ROWS - SPECIES, LANES), jnp.float32)], 0)
    miss = main[0].reshape(ROWS, LANES) - obs
    miss_dot = main_dot[0].reshape(ROWS, LANES)
    square_sum = jnp.sum(miss * miss, 0, keepdims=True)
    cross_sum = jnp.sum(miss * miss_dot, 0, keepdims=True)
    front = lane((1, LANES)) < LANES // 2
    half_row = LANES // 2
    part = jnp.where(front, square_sum + spin(square_sum, half_row), cross_sum + spin(cross_sum, half_row))
    part_out[0] = part
    pl.semaphore_wait(ready, 4 - direct.astype(jnp.int32))

    def straight(across, mid):
        north, east = across // 4, across % 4
        offset = (north - x_hi + 4) % 4 * 4 + (east - y_lo + 4) % 4

        @pl.when(offset > 0)
        def _():
            for core in (1, 0):
                step = (core + x_core) % 2 + (mid - x_mid + 4) % 4 * 2 + y_hi * 8
                partner = north * 8 + mid * 2 + core, jnp.int32(east)
                part_copy(2, part_all.at[offset * 16 - 1 + step], partner).start()

    def along_z(height):
        high, mid = height // 4, height % 4
        for core in (1, 0):
            step = (core + x_core) % 2 + (mid - x_mid + 4) % 4 * 2 + (high + y_hi) % 2 * 8

            @pl.when(step > 0)
            def _(core=core, step=step):
                partner = x_hi * 8 + mid * 2 + core, high * 4 + y_lo
                part_copy(0, part_all.at[step - 1], partner).start()

    straight(0, 0)
    for across in range(4):
        straight(across, 1)
    for height in range(8):
        along_z(height)
    for across in range(1, 16):
        straight(across, 0)
    for across in range(4, 16):
        straight(across, 1)

    shared = miss[8:] + pltpu.roll(miss_dot[8:], 4, 0)
    tiles = [miss[:8], miss_dot[:8], shared]
    for i, tile in enumerate(tiles):
        rim_out[i * 8 : i * 8 + 8] = tile
    rim_strip[0], rim_strip[1] = fold_strips(pack_strips(tiles))
    neighbours(lambda *place: rim_copy(*place).start())

    for dx, column in ADJ_MAIN.items():
        select_table(adj, column, adj_parts, soil_m[dx])
    for dx, column in ADJ_EDGE.items():
        select_table(adj, column, adj_parts, soil_e[dx])

    near, far = part_all.at[pl.ds(0, 15)], part_all.at[pl.ds(15, 240)]

    def all_arrived(buffer, index):
        pltpu.make_async_copy(buffer, buffer, recv_sem.at[2 * len(SEM) + index]).wait()

    @pl.when(jnp.logical_not(direct))
    def _():
        all_arrived(near, 0)
        part_out[1] = part + jnp.sum(part_all[0:15], 0)
        for slot, partner in enumerate(group_b):
            part_copy(1, part_b.at[slot], partner).start()

    arrived(rim_copy)
    lam_m, lam_e, mu_m, mu_e = {}, {}, {}, {}

    def rim_fields(tiles):
        fields = jnp.stack([tiles[0], tiles[2], tiles[1], pltpu.roll(tiles[2], 4, 0)])
        fields = fields.reshape(2, 2, 8, LANES)
        return fields[:1], fields[1:]

    for dx in range(-STEPS, STEPS + 1):
        own = [rim[pl.ds(RIM[dx] + i * 8, 8)] for i in range(3)] if dx else tiles
        lam_m[dx], mu_m[dx] = rim_fields(own)
        if abs(dx) < STEPS:
            left, right = unfold_strips(rim_y[STRIP[dx, -1]], rim_y[STRIP[dx, 1]])
            lam_e[dx], mu_e[dx] = rim_fields([unpack_strip(left, right, i) for i in range(3)])

    sums = {}

    def into(key, value):
        value = value[:, 0] + value[:, 1]
        if key in sums:
            old = sums[key]
            n = old.shape[0]
            sums[key] = jnp.concatenate([old + value[:n], value[n:]], 0) if value.shape[0] > n else old + value
        else:
            sums[key] = value

    own = (("xm", 0), ("xm", -1), ("zm", 0), ("ym", 0), ("ye", 0))
    for k in reversed(range(STEPS)):
        reach = STEPS - 1 - k
        u_m = {dx: mixed(adj, ADJ_MAIN[dx], lam_m[dx]) for dx in lam_m}
        v_m = {dx: mixed(adj, ADJ_MAIN[dx], mu_m[dx]) for dx in mu_m}
        u_e = {dx: mixed(adj, ADJ_EDGE[dx], lam_e[dx]) for dx in lam_e}
        v_e = {dx: mixed(adj, ADJ_EDGE[dx], mu_e[dx]) for dx in mu_e}
        diff_u, diff_v = faces(u_m, u_e, True), faces(v_m, v_e, True)
        for key in own:
            du, dv, dc = diff_u[key], diff_v[key], diffs[k][key][: diff_u[key].shape[0]]
            into(("g", key), du * dc)
            second = dv * dc
            if diffs_dot[k] is not None:
                second = second + du * diffs_dot[k][key][: du.shape[0]]
            into(("h", key), second)
        if k == 0:
            break
        need = lambda diff: {
            key: value for key, value in diff.items()
            if key[0][0] == "x" or abs(key[1]) <= (k if key[0] != "ze" else k - 1)
        }
        diff_u, diff_v = need(diff_u), need(diff_v)
        step_m, step_e = gathered(times(coeff, diff_u), k, True)
        dot_m, dot_e = gathered(plus(times(coeff, diff_v), times(slope, diff_u)), k, True)

        def added(old, step):
            n = old.shape[0]
            return jnp.concatenate([old + step[:n], step[n:]], 0)

        lam_m, lam_e = (
            {dx: added(lam_m[dx], step_m[dx]) for dx in step_m},
            {dx: added(lam_e[dx], step_e[dx]) for dx in step_e},
        )
        mu_m, mu_e = (
            {dx: added(mu_m[dx], dot_m[dx]) for dx in dot_m},
            {dx: added(mu_e[dx], dot_e[dx]) for dx in dot_e},
        )

    def per_cell(name):
        y_sum = sums[name, ("ym", 0)]
        side = sums[name, ("xm", 0)] + sums[name, ("xm", -1)] + y_sum
        side = side + y_prev(y_sum, sums[name, ("ye", 0)])[0]
        depth = sums[name, ("zm", 0)]
        n = side.shape[0]
        total = jnp.concatenate([side + depth[:n] + depth[1:], depth[n:]], 0)
        return jnp.sum(total, 1, keepdims=True)

    weight = weight_m[0][:, 0, :1, :]
    plain_part = -weight * per_cell("g")
    dot_part = -weight * per_cell("h") + own_dire[:, 0, :1, :] * plain_part

    neighbours(lambda *place: halo_copy(*place).wait_send())
    neighbours(lambda *place: rim_copy(*place).wait_send())
    def all_sent(buffer, index):
        pltpu.make_async_copy(buffer, buffer, send_sem.at[2 * len(SEM) + index]).wait()

    all_sent(near, 0)
    all_sent(part_all.at[pl.ds(0, 60)], 2)

    @pl.when(direct)
    def _():
        all_arrived(near, 0)
        all_arrived(far, 2)
        rest = part_all[...].reshape(17, 15, 1, LANES)
        part_sum[...] = part_out[0] + jnp.sum(jnp.sum(rest, 0), 0)

    @pl.when(jnp.logical_not(direct))
    def _():
        all_sent(part_b, 1)
        all_arrived(part_b, 1)
        part_sum[...] = part_out[1] + jnp.sum(part_b[...], 0)

    part = part_sum[...]
    total = jnp.sum(jnp.where(front, part, 0.0), 1, keepdims=True)
    cross = jnp.sum(jnp.where(front, 0.0, part), 1, keepdims=True)
    count = float(SPECIES * nx * ny * LANES)
    factor = count / total
    second = -2.0 * count * cross / (total * total)
    zero = jnp.zeros((1, LANES), jnp.float32)
    for z in range(16):
        one, two = (dot_part[z], plain_part[z]) if z <= STEPS else (zero, zero)
        out_ref[0, z : z + 1, :] = factor * one + second * two


def solution(mesh):
    nx, ny = mesh.shape["gx"], mesh.shape["gy"]

    def body(c_start, log_tort, direction, mix_inverse, pair_mask, soil_layer, observed):
        f32 = jnp.float32
        hbm = pl.BlockSpec(memory_space=pltpu.HBM)
        vmem = pl.BlockSpec(memory_space=pltpu.VMEM)
        return pl.pallas_call(
            lambda *refs: kernel(nx, ny, *refs),
            out_shape=jax.ShapeDtypeStruct((1, 16, LANES), f32),
            in_specs=[hbm] * 7,
            out_specs=vmem,
            scratch_shapes=[
                pltpu.VMEM((ROWS, 8, LANES), f32),
                pltpu.VMEM((1, LANES), jnp.int32),
                pltpu.VMEM((SPECIES, 1, LANES), f32),
                pltpu.VMEM((SPECIES, LAYERS, SPECIES), f32),
                pltpu.VMEM((SPECIES, SPECIES), jnp.int32),
                pltpu.VMEM(((STEPS + 1) * ROWS, LANES), f32),
                pltpu.VMEM((2, 4, LANES), f32),
                pltpu.VMEM((HALO_ROWS, LANES), f32),
                pltpu.VMEM((len(ACROSS), 4, LANES), f32),
                pltpu.VMEM((RIM_ROWS, LANES), f32),
                pltpu.VMEM((2, 4, LANES), f32),
                pltpu.VMEM((len(ALONG_X) * RIM_ROWS, LANES), f32),
                pltpu.VMEM((len(ACROSS), 4, LANES), f32),
                pltpu.VMEM((2, 1, LANES), f32),
                pltpu.VMEM((255, 1, LANES), f32),
                pltpu.VMEM((15, 1, LANES), f32),
                pltpu.VMEM((1, LANES), f32),
                pltpu.VMEM((LANES, LANES), f32),
                pltpu.VMEM((LAYERS, SPECIES, 2, 8, LANES), f32),
                pltpu.VMEM((LAYERS, SPECIES, 2, 8, LANES), f32),
                pltpu.VMEM((8, SPECIES, 2, 8, LANES), f32),
                pltpu.VMEM((12, SPECIES, 2, 8, LANES), f32),
                pltpu.SemaphoreType.DMA((7,)),
                pltpu.SemaphoreType.DMA((2 * len(SEM) + 3,)),
                pltpu.SemaphoreType.DMA((2 * len(SEM) + 3,)),
                pltpu.SemaphoreType.REGULAR,
            ],
            compiler_params=pltpu.CompilerParams(
                collective_id=0, has_side_effects=True, vmem_limit_bytes=32 * 1024 * 1024
            ),
        )(*(
            pltpu.with_memory_space_constraint(value, pltpu.HBM)
            for value in (
                c_start, log_tort, direction, mix_inverse.transpose(1, 0, 2), pair_mask, soil_layer, observed,
            )
        ))

    return jax.shard_map(
        body,
        mesh=mesh,
        in_specs=(
            P(None, "gx", None, "gy"),
            P("gx", None, "gy"),
            P("gx", None, "gy"),
            P(),
            P(),
            P("gx", "gy"),
            P(None, "gx", "gy"),
        ),
        out_specs=P("gx", None, "gy"),
        check_vma=False,
    )
```

```python
import jax
import jax.numpy as jnp
from jax import lax
from jax.experimental import pallas as pl
from jax.experimental.pallas import tpu as pltpu
from jax.sharding import PartitionSpec as P

MESH = pl.DeviceIdType.MESH
DT = 0.04
STEPS = 3
SPECIES = 12
LAYERS = 4
LANES = 128
ROWS = 16
TORT, DIRE, SOIL = 12, 13, 14


def offsets():
    found = []
    for dx in range(-STEPS, STEPS + 1):
        for dy in (-1, 0, 1):
            depths = STEPS + 1 - abs(dx) - (1 if dy else 0)
            if depths > 0 and (dx or dy):
                found.append((dx, dy, depths))
    return found


ALONG_X = [(dx, dy, depths) for dx, dy, depths in offsets() if dy == 0]
ACROSS = [(dx, dy) for dx, dy, _ in offsets() if dy]
STRIP = {place: i for i, place in enumerate(ACROSS)}
SEM = {(dx, dy): i for i, (dx, dy, _) in enumerate(offsets())}
HALO, HALO_ROWS = {}, 0
for dx, _, depths in ALONG_X:
    HALO[dx] = HALO_ROWS
    HALO_ROWS += depths * ROWS
RIM_ROWS = 24
RIM = {dx: i * RIM_ROWS for i, (dx, _, _) in enumerate(ALONG_X)}
FWD_MAIN = {dx: i for i, dx in enumerate(range(-2, 3))}
FWD_EDGE = {dx: 5 + i for i, dx in enumerate(range(-1, 2))}
ADJ_MAIN = {dx: i for i, dx in enumerate(range(-3, 4))}
ADJ_EDGE = {dx: 7 + i for i, dx in enumerate(range(-2, 3))}


def lane(shape):
    return lax.broadcasted_iota(jnp.int32, shape, len(shape) - 1)


def spin(value, by):
    return pltpu.roll(value, by % LANES, value.ndim - 1)


def y_next(main, edge):
    last = lane(main.shape) == LANES - 1
    a, b = spin(main, -1), spin(edge, -1)
    return jnp.where(last, b, a), jnp.where(last, a, b)


def y_prev(main, edge):
    first = lane(main.shape) == 0
    a, b = spin(main, 1), spin(edge, 1)
    return jnp.where(first, b, a), jnp.where(first, a, b)


def pack_strips(tiles):
    group = lane((8, LANES)) // 8
    packed = tiles[0]
    for i, tile in enumerate(tiles[1:], 1):
        packed = jnp.where(group == i, spin(tile, 8 * i), packed)
        packed = jnp.where(group == 15 - i, spin(tile, -8 * i), packed)
    return packed


FOLD = 48


def fold_strips(packed):
    place = lane((8, LANES))
    last = jnp.where(place >= LANES - FOLD, packed, pltpu.roll(spin(packed, -FOLD), 4, 0))
    first = jnp.where(place < FOLD, packed, pltpu.roll(spin(packed, FOLD), 4, 0))
    return last[:4], first[:4]


def unfold_strips(left, right):
    return jnp.concatenate([left, spin(left, FOLD)], 0), jnp.concatenate([right, spin(right, -FOLD)], 0)


def unpack_strip(left, right, i):
    return jnp.where(lane((8, LANES)) < LANES // 2, spin(right, -8 * i), spin(left, 8 * i))


def faces(main, edge, closed):
    out = {}
    for kind, field in (("m", main), ("e", edge)):
        for dx in field:
            value = field[dx]
            if dx + 1 in field:
                n = min(value.shape[0], field[dx + 1].shape[0])
                out["x" + kind, dx] = field[dx + 1][:n] - value[:n]
            parts = [value[:1]]
            if value.shape[0] > 1:
                parts.append(value[1:] - value[:-1])
            if closed:
                parts.append(-value[-1:])
            out["z" + kind, dx] = jnp.concatenate(parts, 0) if len(parts) > 1 else parts[0]
    for dx in edge:
        n = edge[dx].shape[0]
        a, b = y_next(main[dx][:n], edge[dx][:n])
        out["ym", dx] = a - main[dx][:n]
        out["ye", dx] = b - edge[dx][:n]
    return out


def times(coeff, diff):
    return {key: coeff[key][: diff[key].shape[0]] * diff[key] for key in diff}


def plus(one, two):
    return {key: one[key] + two[key] for key in one}


def gathered(flux, reach, closed):
    result = []
    for kind, most in (("m", reach), ("e", reach - 1)):
        field = {}
        for dx in range(-most, most + 1):
            depth = flux["z" + kind, dx]
            n = depth.shape[0] - 1
            total = depth[1:] - depth[:-1]
            a, b = y_prev(flux["ym", dx], flux["ye", dx])
            back = a if kind == "m" else b
            side = (
                flux["x" + kind, dx][:n]
                - flux["x" + kind, dx - 1][:n]
                + flux["y" + kind, dx][:n]
                - back[:n]
            )
            if closed:
                total = jnp.concatenate([total[:n] + side, -depth[n:]], 0)
            else:
                total = total + side
            field[dx] = total
        result.append(field)
    return result


def mixed(table, column, value):
    total = None
    for t in range(SPECIES):
        part = table[column, t] * value[:, t // 8 : t // 8 + 1, t % 8 : t % 8 + 1, :]
        total = part if total is None else total + part
    return total


def select_table(table, column, parts, soil):
    masks = [soil == float(level) for level in range(LAYERS)]
    for t in range(SPECIES):
        for half in range(2):
            value = jnp.zeros((8, LANES), jnp.float32)
            for level in range(LAYERS):
                value = jnp.where(masks[level], parts[level, t, half], value)
            table[column, t, half] = value


def kernel(
    nx, ny, c_hbm, m_hbm, d_hbm, mix_hbm, pair_hbm, soil_hbm, obs_hbm, out_ref,
    stage, soil_v, obs_v, mix_ref, pair_ref, block, strip, halo, halo_y, rim_out, rim_strip, rim, rim_y,
    part_out, part_all, part_b, part_sum,
    square, fwd_parts, adj_parts, fwd, adj,
    local_sem, send_sem, recv_sem, ready,
):
    x, y = lax.axis_index("gx"), lax.axis_index("gy")
    x_hi, x_mid, x_core = x // 8, (x // 2) % 4, x % 2
    y_hi, y_lo = y // 4, y % 4

    in_x = {dx: jnp.logical_and(x + dx >= 0, x + dx < nx) for dx in range(-STEPS, STEPS + 1)}
    all_in_x = jnp.logical_and(x >= STEPS, x < nx - STEPS)

    def neighbours(act, rows=(-1, 1, 0)):
        for dy in rows:
            places = [place for place in offsets() if place[1] == dy]

            def row(places=places):
                @pl.when(all_in_x)
                def _():
                    for place in places:
                        act(*place)

                @pl.when(jnp.logical_not(all_in_x))
                def _():
                    for place in places:
                        pl.when(in_x[place[0]])(lambda place=place: act(*place))

            if dy:
                pl.when(y > 0 if dy < 0 else y < ny - 1)(row)
            else:
                row()

    def signal(semaphore, partner):
        pl.semaphore_signal(semaphore, inc=1, device_id=partner, device_id_type=MESH)

    loads = [
        pltpu.make_async_copy(c_hbm.at[:, 0, 0:8], stage.at[0:SPECIES], local_sem.at[0]),
        pltpu.make_async_copy(m_hbm.at[0, 0:8], stage.at[TORT], local_sem.at[1]),
        pltpu.make_async_copy(d_hbm.at[0, 0:8], stage.at[DIRE], local_sem.at[2]),
        pltpu.make_async_copy(soil_hbm, soil_v, local_sem.at[3]),
        pltpu.make_async_copy(mix_hbm, mix_ref, local_sem.at[4]),
        pltpu.make_async_copy(pair_hbm, pair_ref, local_sem.at[5]),
        pltpu.make_async_copy(obs_hbm, obs_v, local_sem.at[6]),
    ]
    rim[...] = jnp.zeros_like(rim)
    rim_y[...] = jnp.zeros_like(rim_y)
    barrier = pltpu.get_barrier_semaphore()
    neighbours(lambda dx, dy, _: signal(barrier, (x + dx, y + dy)))
    for copy in loads:
        copy.start()
    group_a = []
    for i in range(1, 16):
        core, mid, high = i % 2, (i // 2) % 4, i // 8
        group_a.append((x_hi * 8 + (x_mid + mid) % 4 * 2 + (x_core + core) % 2, (y_hi + high) % 2 * 4 + y_lo))
    group_b = []
    for i in range(1, 16):
        group_b.append(((x_hi + i // 4) % 4 * 8 + x_mid * 2 + x_core, y_hi * 4 + (y_lo + i % 4) % 4))
    direct = jnp.logical_and(y_hi == 0, x_mid < 2)
    for partner in group_a + group_b:
        signal(barrier, partner)
    arrivals = len(group_a + group_b)
    for dx, dy, _ in offsets():
        there = in_x[dx]
        if dy:
            there = jnp.logical_and(there, y > 0 if dy < 0 else y < ny - 1)
        arrivals = arrivals + there.astype(jnp.int32)

    stage[SOIL] = jnp.zeros((8, LANES), jnp.float32)
    stage[SOIL + 1] = jnp.zeros((8, LANES), jnp.float32)
    for copy in loads[:4]:
        copy.wait()
    stage[SOIL, 0:1] = soil_v[...].astype(jnp.float32)
    flat = stage.reshape((ROWS + 1) * 8, LANES)
    for z in range(STEPS + 1):
        for half in range(2):
            block[pl.ds(z * ROWS + half * 8, 8)] = flat[pl.ds(half * 64 + z, 8, stride=8)]
    strip[0], strip[1] = fold_strips(pack_strips([block[i * 8 : i * 8 + 8] for i in range(2 * STEPS)]))

    pl.semaphore_wait(barrier, arrivals)

    @pl.when(direct)
    def _():
        for partner in group_a:
            signal(ready, partner)


    def copy_of(src, dst, sems, number, partner):
        return pltpu.make_async_remote_copy(
            src_ref=src, dst_ref=dst, send_sem=send_sem.at[sems + number], recv_sem=recv_sem.at[sems + number],
            device_id=partner, device_id_type=MESH,
        )

    def halo_copy(dx, dy, depths):
        if dy:
            src, dst = strip.at[(1 - dy) // 2], halo_y.at[STRIP[-dx, -dy]]
        else:
            src, dst = block.at[pl.ds(0, depths * ROWS)], halo.at[pl.ds(HALO[-dx], depths * ROWS)]
        return copy_of(src, dst, 0, SEM[-dx, -dy], (x + dx, y + dy))

    def rim_copy(dx, dy, _):
        if dy:
            src, dst = rim_strip.at[(1 - dy) // 2], rim_y.at[STRIP[-dx, -dy]]
        else:
            src, dst = rim_out, rim.at[pl.ds(RIM[-dx], RIM_ROWS)]
        return copy_of(src, dst, len(SEM), SEM[-dx, -dy], (x + dx, y + dy))

    def part_copy(index, dst, partner):
        return copy_of(part_out.at[index % 2], dst, 2 * len(SEM), index, partner)

    neighbours(lambda *place: halo_copy(*place).start(), (-1, 1))

    def along(places):
        @pl.when(all_in_x)
        def _():
            for place in places:
                halo_copy(*place).start()

        @pl.when(jnp.logical_not(all_in_x))
        def _():
            for place in places:
                pl.when(in_x[place[0]])(lambda place=place: halo_copy(*place).start())

    pl.when(x % 8 < 4)(lambda: along(ALONG_X))
    pl.when(x % 8 >= 4)(lambda: along(ALONG_X[::-1]))

    for copy in loads[4:]:
        copy.wait()
    square[...] = jnp.zeros((LANES, LANES), jnp.float32)
    diagonal = lax.broadcasted_iota(jnp.int32, (SPECIES, SPECIES), 0) == lax.broadcasted_iota(
        jnp.int32, (SPECIES, SPECIES), 1
    )
    pair = pair_ref[...].astype(jnp.float32)
    for level in range(LAYERS):
        entry = mix_ref[:, level, :]
        square[level * ROWS : level * ROWS + SPECIES, 0:SPECIES] = jnp.where(diagonal, entry, entry * pair)
    plain = square[...]
    turned = plain.T
    for level in range(LAYERS):
        for t in range(SPECIES):
            for half in range(2):
                row = level * ROWS + half * 8
                fwd_parts[level, t, half] = jnp.broadcast_to(plain[row : row + 8, t : t + 1], (8, LANES))
                col = level * ROWS + t
                adj_parts[level, t, half] = jnp.broadcast_to(
                    turned[half * 8 : half * 8 + 8, col : col + 1], (8, LANES)
                )

    def arrived(copy, rows=(-1, 1, 0)):
        def act(dx, dy, depths):
            copy(-dx, -dy, depths).wait_recv()
        neighbours(act, rows)

    species_row = lax.broadcasted_iota(jnp.int32, (1, 2, 8, LANES), 1) * 8 + lax.broadcasted_iota(
        jnp.int32, (1, 2, 8, LANES), 2
    )
    right_half = lane((8, LANES)) < LANES // 2
    in_y = jnp.where(right_half, y + 1, y - 1)
    in_y = jnp.logical_and(in_y >= 0, in_y < ny)

    def cells(ref, start, depths):
        return ref[pl.ds(start, depths * ROWS)].reshape(depths, 2, 8, LANES)

    def row_of(value, row):
        depths = value.shape[0]
        return jnp.broadcast_to(value[:, row // 8, row % 8 : row % 8 + 1, :], (depths, 8, LANES))

    def zero_unless(valid, value):
        return jnp.where(jnp.broadcast_to(valid, value.shape), value, 0.0)

    def unpack(value, valid):
        depths = value.shape[0]
        state = jnp.where(jnp.broadcast_to(species_row < SPECIES, value.shape), value, 0.0)
        tort, dire = row_of(value, TORT), row_of(value, DIRE)
        soil = row_of(value[:1], SOIL)[0]
        if valid is not None:
            state = zero_unless(valid, state)
            tort, dire = zero_unless(valid, tort), zero_unless(valid, dire)
            soil = jnp.where(valid, soil, -1.0)
        weight = (0.5 * DT) * jnp.exp(tort)
        turn = weight * dire
        shape = (depths, 1, 8, LANES)
        return state, weight.reshape(shape), turn.reshape(shape), dire.reshape(shape), soil

    main, edge = {}, {}
    weight_m, weight_e, turn_m, turn_e, soil_m, soil_e = {}, {}, {}, {}, {}, {}
    main[0], weight_m[0], turn_m[0], own_dire, soil_m[0] = unpack(cells(block, 0, STEPS + 1), None)
    select_table(fwd, FWD_MAIN[0], fwd_parts, soil_m[0])

    arrived(halo_copy, (-1, 1))
    for dx in range(1 - STEPS, STEPS):
        depths = STEPS - abs(dx)
        left, right = unfold_strips(halo_y[STRIP[dx, -1]], halo_y[STRIP[dx, 1]])
        raw = jnp.stack([unpack_strip(left, right, i) for i in range(2 * depths)])
        valid = jnp.logical_and(in_y, jnp.broadcast_to(in_x[dx], (8, LANES)))
        edge[dx], weight_e[dx], turn_e[dx], _, soil_e[dx] = unpack(raw.reshape(depths, 2, 8, LANES), valid)
    for dx, column in FWD_EDGE.items():
        select_table(fwd, column, fwd_parts, soil_e[dx])

    arrived(halo_copy, (0,))
    for dx, _, depths in ALONG_X:
        valid = jnp.broadcast_to(in_x[dx], (8, LANES))
        main[dx], weight_m[dx], turn_m[dx], _, soil_m[dx] = unpack(cells(halo, HALO[dx], depths), valid)
    main, weight_m, turn_m = ({dx: field[dx] for dx in sorted(field)} for field in (main, weight_m, turn_m))
    for dx, column in FWD_MAIN.items():
        if dx:
            select_table(fwd, column, fwd_parts, soil_m[dx])

    def face_sums(main_w, edge_w, outside):
        out = {}
        for kind, field in (("m", main_w), ("e", edge_w)):
            for dx in field:
                value = field[dx]
                if dx + 1 in field:
                    n = min(value.shape[0], field[dx + 1].shape[0])
                    out["x" + kind, dx] = field[dx + 1][:n] + value[:n]
                parts = [value[:1] + outside]
                if value.shape[0] > 1:
                    parts.append(value[1:] + value[:-1])
                out["z" + kind, dx] = jnp.concatenate(parts, 0) if len(parts) > 1 else parts[0]
        for dx in edge_w:
            n = edge_w[dx].shape[0]
            a, b = y_next(main_w[dx][:n], edge_w[dx][:n])
            out["ym", dx] = a + main_w[dx][:n]
            out["ye", dx] = b + edge_w[dx][:n]
        return out

    coeff = face_sums(weight_m, weight_e, 0.5 * DT)
    slope = face_sums(turn_m, turn_e, 0.0)

    diffs, diffs_dot = [], []
    main_dot, edge_dot = None, None
    for k in range(STEPS):
        reach = STEPS - 1 - k
        diff = faces(main, edge, False)
        diffs.append(diff)
        flux = times(coeff, diff)
        flux_dot = times(slope, diff)
        if main_dot is not None:
            diff_dot = faces(main_dot, edge_dot, False)
            flux_dot = plus(flux_dot, times(coeff, diff_dot))
        else:
            diff_dot = None
        diffs_dot.append(diff_dot)
        spread_m, spread_e = gathered(flux, reach, False)
        dot_m, dot_e = gathered(flux_dot, reach, False)
        new = [{}, {}, {}, {}]
        for kind, table, old, old_dot, spread, dot in (
            (0, FWD_MAIN, main, main_dot, spread_m, dot_m),
            (1, FWD_EDGE, edge, edge_dot, spread_e, dot_e),
        ):
            for dx in spread:
                n = spread[dx].shape[0]
                new[kind][dx] = old[dx][:n] + mixed(fwd, table[dx], spread[dx])
                moved = mixed(fwd, table[dx], dot[dx])
                new[2 + kind][dx] = moved if old_dot is None else old_dot[dx][:n] + moved
        main, edge, main_dot, edge_dot = new

    obs = jnp.concatenate([obs_v[s] for s in range(SPECIES)] + [jnp.zeros((ROWS - SPECIES, LANES), jnp.float32)], 0)
    miss = main[0].reshape(ROWS, LANES) - obs
    miss_dot = main_dot[0].reshape(ROWS, LANES)
    square_sum = jnp.sum(miss * miss, 0, keepdims=True)
    cross_sum = jnp.sum(miss * miss_dot, 0, keepdims=True)
    front = lane((1, LANES)) < LANES // 2
    half_row = LANES // 2
    part = jnp.where(front, square_sum + spin(square_sum, half_row), cross_sum + spin(cross_sum, half_row))
    part_out[0] = part
    pl.semaphore_wait(ready, 4 - direct.astype(jnp.int32))

    def straight(across, mid):
        north, east = across // 4, across % 4
        offset = (north - x_hi + 4) % 4 * 4 + (east - y_lo + 4) % 4

        @pl.when(offset > 0)
        def _():
            for core in (1, 0):
                step = (core + x_core) % 2 + (mid - x_mid + 4) % 4 * 2 + y_hi * 8
                partner = north * 8 + mid * 2 + core, jnp.int32(east)
                part_copy(2, part_all.at[offset * 16 - 1 + step], partner).start()

    def along_z(height):
        high, mid = height // 4, height % 4
        for core in (1, 0):
            step = (core + x_core) % 2 + (mid - x_mid + 4) % 4 * 2 + (high + y_hi) % 2 * 8

            @pl.when(step > 0)
            def _(core=core, step=step):
                partner = x_hi * 8 + mid * 2 + core, high * 4 + y_lo
                part_copy(0, part_all.at[step - 1], partner).start()

    straight(0, 0)
    for across in range(4):
        straight(across, 1)
    for height in range(8):
        along_z(height)
    for across in range(1, 16):
        straight(across, 0)
    for across in range(4, 16):
        straight(across, 1)

    shared = miss[8:] + pltpu.roll(miss_dot[8:], 4, 0)
    tiles = [miss[:8], miss_dot[:8], shared]
    for i, tile in enumerate(tiles):
        rim_out[i * 8 : i * 8 + 8] = tile
    rim_strip[0], rim_strip[1] = fold_strips(pack_strips(tiles))
    neighbours(lambda *place: rim_copy(*place).start())

    for dx, column in ADJ_MAIN.items():
        select_table(adj, column, adj_parts, soil_m[dx])
    for dx, column in ADJ_EDGE.items():
        select_table(adj, column, adj_parts, soil_e[dx])

    near, far = part_all.at[pl.ds(0, 15)], part_all.at[pl.ds(15, 240)]

    def all_arrived(buffer, index):
        pltpu.make_async_copy(buffer, buffer, recv_sem.at[2 * len(SEM) + index]).wait()

    @pl.when(jnp.logical_not(direct))
    def _():
        all_arrived(near, 0)
        part_out[1] = part + jnp.sum(part_all[0:15], 0)
        for slot, partner in enumerate(group_b):
            part_copy(1, part_b.at[slot], partner).start()

    arrived(rim_copy)
    lam_m, lam_e, mu_m, mu_e = {}, {}, {}, {}

    def rim_fields(tiles):
        fields = jnp.stack([tiles[0], tiles[2], tiles[1], pltpu.roll(tiles[2], 4, 0)])
        fields = fields.reshape(2, 2, 8, LANES)
        return fields[:1], fields[1:]

    for dx in range(-STEPS, STEPS + 1):
        own = [rim[pl.ds(RIM[dx] + i * 8, 8)] for i in range(3)] if dx else tiles
        lam_m[dx], mu_m[dx] = rim_fields(own)
        if abs(dx) < STEPS:
            left, right = unfold_strips(rim_y[STRIP[dx, -1]], rim_y[STRIP[dx, 1]])
            lam_e[dx], mu_e[dx] = rim_fields([unpack_strip(left, right, i) for i in range(3)])

    sums = {}

    def into(key, value):
        value = value[:, 0] + value[:, 1]
        if key in sums:
            old = sums[key]
            n = old.shape[0]
            sums[key] = jnp.concatenate([old + value[:n], value[n:]], 0) if value.shape[0] > n else old + value
        else:
            sums[key] = value

    own = (("xm", 0), ("xm", -1), ("zm", 0), ("ym", 0), ("ye", 0))
    for k in reversed(range(STEPS)):
        reach = STEPS - 1 - k
        u_m = {dx: mixed(adj, ADJ_MAIN[dx], lam_m[dx]) for dx in lam_m}
        v_m = {dx: mixed(adj, ADJ_MAIN[dx], mu_m[dx]) for dx in mu_m}
        u_e = {dx: mixed(adj, ADJ_EDGE[dx], lam_e[dx]) for dx in lam_e}
        v_e = {dx: mixed(adj, ADJ_EDGE[dx], mu_e[dx]) for dx in mu_e}
        diff_u, diff_v = faces(u_m, u_e, True), faces(v_m, v_e, True)
        for key in own:
            du, dv, dc = diff_u[key], diff_v[key], diffs[k][key][: diff_u[key].shape[0]]
            into(("g", key), du * dc)
            second = dv * dc
            if diffs_dot[k] is not None:
                second = second + du * diffs_dot[k][key][: du.shape[0]]
            into(("h", key), second)
        if k == 0:
            break
        need = lambda diff: {
            key: value for key, value in diff.items()
            if key[0][0] == "x" or abs(key[1]) <= (k if key[0] != "ze" else k - 1)
        }
        diff_u, diff_v = need(diff_u), need(diff_v)
        step_m, step_e = gathered(times(coeff, diff_u), k, True)
        dot_m, dot_e = gathered(plus(times(coeff, diff_v), times(slope, diff_u)), k, True)

        def added(old, step):
            n = old.shape[0]
            return jnp.concatenate([old + step[:n], step[n:]], 0)

        lam_m, lam_e = (
            {dx: added(lam_m[dx], step_m[dx]) for dx in step_m},
            {dx: added(lam_e[dx], step_e[dx]) for dx in step_e},
        )
        mu_m, mu_e = (
            {dx: added(mu_m[dx], dot_m[dx]) for dx in dot_m},
            {dx: added(mu_e[dx], dot_e[dx]) for dx in dot_e},
        )

    def per_cell(name):
        y_sum = sums[name, ("ym", 0)]
        side = sums[name, ("xm", 0)] + sums[name, ("xm", -1)] + y_sum
        side = side + y_prev(y_sum, sums[name, ("ye", 0)])[0]
        depth = sums[name, ("zm", 0)]
        n = side.shape[0]
        total = jnp.concatenate([side + depth[:n] + depth[1:], depth[n:]], 0)
        return jnp.sum(total, 1, keepdims=True)

    weight = weight_m[0][:, 0, :1, :]
    plain_part = -weight * per_cell("g")
    dot_part = -weight * per_cell("h") + own_dire[:, 0, :1, :] * plain_part

    neighbours(lambda *place: halo_copy(*place).wait_send())
    neighbours(lambda *place: rim_copy(*place).wait_send())
    def all_sent(buffer, index):
        pltpu.make_async_copy(buffer, buffer, send_sem.at[2 * len(SEM) + index]).wait()

    all_sent(near, 0)
    all_sent(part_all.at[pl.ds(0, 60)], 2)

    @pl.when(direct)
    def _():
        all_arrived(near, 0)
        all_arrived(far, 2)
        rest = part_all[...].reshape(17, 15, 1, LANES)
        part_sum[...] = part_out[0] + jnp.sum(jnp.sum(rest, 0), 0)

    @pl.when(jnp.logical_not(direct))
    def _():
        all_sent(part_b, 1)
        all_arrived(part_b, 1)
        part_sum[...] = part_out[1] + jnp.sum(part_b[...], 0)

    part = part_sum[...]
    total = jnp.sum(jnp.where(front, part, 0.0), 1, keepdims=True)
    cross = jnp.sum(jnp.where(front, 0.0, part), 1, keepdims=True)
    count = float(SPECIES * nx * ny * LANES)
    factor = count / total
    second = -2.0 * count * cross / (total * total)
    zero = jnp.zeros((1, LANES), jnp.float32)
    for z in range(16):
        one, two = (dot_part[z], plain_part[z]) if z <= STEPS else (zero, zero)
        out_ref[0, z : z + 1, :] = factor * one + second * two


def solution(mesh):
    nx, ny = mesh.shape["gx"], mesh.shape["gy"]

    def body(c_start, log_tort, direction, mix_inverse, pair_mask, soil_layer, observed):
        f32 = jnp.float32
        hbm = pl.BlockSpec(memory_space=pltpu.HBM)
        vmem = pl.BlockSpec(memory_space=pltpu.VMEM)
        return pl.pallas_call(
            lambda *refs: kernel(nx, ny, *refs),
            out_shape=jax.ShapeDtypeStruct((1, 16, LANES), f32),
            in_specs=[hbm] * 7,
            out_specs=vmem,
            scratch_shapes=[
                pltpu.VMEM((ROWS + 1, 8, LANES), f32),
                pltpu.VMEM((1, LANES), jnp.int32),
                pltpu.VMEM((SPECIES, 1, LANES), f32),
                pltpu.VMEM((SPECIES, LAYERS, SPECIES), f32),
                pltpu.VMEM((SPECIES, SPECIES), jnp.int32),
                pltpu.VMEM(((STEPS + 1) * ROWS, LANES), f32),
                pltpu.VMEM((2, 4, LANES), f32),
                pltpu.VMEM((HALO_ROWS, LANES), f32),
                pltpu.VMEM((len(ACROSS), 4, LANES), f32),
                pltpu.VMEM((RIM_ROWS, LANES), f32),
                pltpu.VMEM((2, 4, LANES), f32),
                pltpu.VMEM((len(ALONG_X) * RIM_ROWS, LANES), f32),
                pltpu.VMEM((len(ACROSS), 4, LANES), f32),
                pltpu.VMEM((2, 1, LANES), f32),
                pltpu.VMEM((255, 1, LANES), f32),
                pltpu.VMEM((15, 1, LANES), f32),
                pltpu.VMEM((1, LANES), f32),
                pltpu.VMEM((LANES, LANES), f32),
                pltpu.VMEM((LAYERS, SPECIES, 2, 8, LANES), f32),
                pltpu.VMEM((LAYERS, SPECIES, 2, 8, LANES), f32),
                pltpu.VMEM((8, SPECIES, 2, 8, LANES), f32),
                pltpu.VMEM((12, SPECIES, 2, 8, LANES), f32),
                pltpu.SemaphoreType.DMA((7,)),
                pltpu.SemaphoreType.DMA((2 * len(SEM) + 3,)),
                pltpu.SemaphoreType.DMA((2 * len(SEM) + 3,)),
                pltpu.SemaphoreType.REGULAR,
            ],
            compiler_params=pltpu.CompilerParams(
                collective_id=0, has_side_effects=True, vmem_limit_bytes=32 * 1024 * 1024
            ),
        )(*(
            pltpu.with_memory_space_constraint(value, pltpu.HBM)
            for value in (
                c_start, log_tort, direction, mix_inverse.transpose(1, 0, 2), pair_mask, soil_layer, observed,
            )
        ))

    return jax.shard_map(
        body,
        mesh=mesh,
        in_specs=(
            P(None, "gx", None, "gy"),
            P("gx", None, "gy"),
            P("gx", None, "gy"),
            P(),
            P(),
            P("gx", "gy"),
            P(None, "gx", "gy"),
        ),
        out_specs=P("gx", None, "gy"),
        check_vma=False,
    )
```

```python
import jax
import jax.numpy as jnp
from jax import lax
from jax.experimental import pallas as pl
from jax.experimental.pallas import tpu as pltpu
from jax.sharding import PartitionSpec as P

MESH = pl.DeviceIdType.MESH
DT = 0.04
STEPS = 3
SPECIES = 12
LAYERS = 4
LANES = 128
ROWS = 16
TORT, DIRE, SOIL = 12, 13, 14


def offsets():
    found = []
    for dx in range(-STEPS, STEPS + 1):
        for dy in (-1, 0, 1):
            depths = STEPS + 1 - abs(dx) - (1 if dy else 0)
            if depths > 0 and (dx or dy):
                found.append((dx, dy, depths))
    return found


ALONG_X = [(dx, dy, depths) for dx, dy, depths in offsets() if dy == 0]
ACROSS = [(dx, dy) for dx, dy, _ in offsets() if dy]
STRIP = {place: i for i, place in enumerate(ACROSS)}
SEM = {(dx, dy): i for i, (dx, dy, _) in enumerate(offsets())}
HALO, HALO_ROWS = {}, 0
for dx, _, depths in ALONG_X:
    HALO[dx] = HALO_ROWS
    HALO_ROWS += depths * ROWS
RIM_ROWS = 24
RIM = {dx: i * RIM_ROWS for i, (dx, _, _) in enumerate(ALONG_X)}
FWD_MAIN = {dx: i for i, dx in enumerate(range(-2, 3))}
FWD_EDGE = {dx: 5 + i for i, dx in enumerate(range(-1, 2))}
ADJ_MAIN = {dx: i for i, dx in enumerate(range(-3, 4))}
ADJ_EDGE = {dx: 7 + i for i, dx in enumerate(range(-2, 3))}


def lane(shape):
    return lax.broadcasted_iota(jnp.int32, shape, len(shape) - 1)


def spin(value, by):
    return pltpu.roll(value, by % LANES, value.ndim - 1)


def y_next(main, edge):
    last = lane(main.shape) == LANES - 1
    a, b = spin(main, -1), spin(edge, -1)
    return jnp.where(last, b, a), jnp.where(last, a, b)


def y_prev(main, edge):
    first = lane(main.shape) == 0
    a, b = spin(main, 1), spin(edge, 1)
    return jnp.where(first, b, a), jnp.where(first, a, b)


def pack_strips(tiles):
    group = lane((8, LANES)) // 8
    packed = tiles[0]
    for i, tile in enumerate(tiles[1:], 1):
        packed = jnp.where(group == i, spin(tile, 8 * i), packed)
        packed = jnp.where(group == 15 - i, spin(tile, -8 * i), packed)
    return packed


FOLD = 48


def fold_strips(packed):
    place = lane((8, LANES))
    last = jnp.where(place >= LANES - FOLD, packed, pltpu.roll(spin(packed, -FOLD), 4, 0))
    first = jnp.where(place < FOLD, packed, pltpu.roll(spin(packed, FOLD), 4, 0))
    return last[:4], first[:4]


def unfold_strips(left, right):
    return jnp.concatenate([left, spin(left, FOLD)], 0), jnp.concatenate([right, spin(right, -FOLD)], 0)


def unpack_strip(left, right, i):
    return jnp.where(lane((8, LANES)) < LANES // 2, spin(right, -8 * i), spin(left, 8 * i))


def faces(main, edge, closed):
    out = {}
    for kind, field in (("m", main), ("e", edge)):
        for dx in field:
            value = field[dx]
            if dx + 1 in field:
                n = min(value.shape[0], field[dx + 1].shape[0])
                out["x" + kind, dx] = field[dx + 1][:n] - value[:n]
            parts = [value[:1]]
            if value.shape[0] > 1:
                parts.append(value[1:] - value[:-1])
            if closed:
                parts.append(-value[-1:])
            out["z" + kind, dx] = jnp.concatenate(parts, 0) if len(parts) > 1 else parts[0]
    for dx in edge:
        n = edge[dx].shape[0]
        a, b = y_next(main[dx][:n], edge[dx][:n])
        out["ym", dx] = a - main[dx][:n]
        out["ye", dx] = b - edge[dx][:n]
    return out


def times(coeff, diff):
    return {key: coeff[key][: diff[key].shape[0]] * diff[key] for key in diff}


def plus(one, two):
    return {key: one[key] + two[key] for key in one}


def gathered(flux, reach, closed):
    result = []
    for kind, most in (("m", reach), ("e", reach - 1)):
        field = {}
        for dx in range(-most, most + 1):
            depth = flux["z" + kind, dx]
            n = depth.shape[0] - 1
            total = depth[1:] - depth[:-1]
            a, b = y_prev(flux["ym", dx], flux["ye", dx])
            back = a if kind == "m" else b
            side = (
                flux["x" + kind, dx][:n]
                - flux["x" + kind, dx - 1][:n]
                + flux["y" + kind, dx][:n]
                - back[:n]
            )
            if closed:
                total = jnp.concatenate([total[:n] + side, -depth[n:]], 0)
            else:
                total = total + side
            field[dx] = total
        result.append(field)
    return result


def mixed(table, column, value):
    total = None
    for t in range(SPECIES):
        part = table[column, t] * value[:, t // 8 : t // 8 + 1, t % 8 : t % 8 + 1, :]
        total = part if total is None else total + part
    return total


def select_table(table, column, parts, soil):
    masks = [soil == float(level) for level in range(LAYERS)]
    for t in range(SPECIES):
        for half in range(2):
            value = jnp.zeros((8, LANES), jnp.float32)
            for level in range(LAYERS):
                value = jnp.where(masks[level], parts[level, t, half], value)
            table[column, t, half] = value


def kernel(
    nx, ny, c_hbm, m_hbm, d_hbm, mix_hbm, pair_hbm, soil_hbm, obs_hbm, out_ref,
    stage, soil_v, obs_v, mix_ref, pair_ref, block, strip, halo, halo_y, rim_out, rim_strip, rim, rim_y,
    part_out, part_all, part_b, part_sum,
    square, fwd_parts, adj_parts, fwd, adj,
    local_sem, send_sem, recv_sem, ready,
):
    x, y = lax.axis_index("gx"), lax.axis_index("gy")
    x_hi, x_mid, x_core = x // 8, (x // 2) % 4, x % 2
    y_hi, y_lo = y // 4, y % 4

    in_x = {dx: jnp.logical_and(x + dx >= 0, x + dx < nx) for dx in range(-STEPS, STEPS + 1)}
    all_in_x = jnp.logical_and(x >= STEPS, x < nx - STEPS)

    def neighbours(act, rows=(-1, 1, 0)):
        for dy in rows:
            places = [place for place in offsets() if place[1] == dy]

            def row(places=places):
                @pl.when(all_in_x)
                def _():
                    for place in places:
                        act(*place)

                @pl.when(jnp.logical_not(all_in_x))
                def _():
                    for place in places:
                        pl.when(in_x[place[0]])(lambda place=place: act(*place))

            if dy:
                pl.when(y > 0 if dy < 0 else y < ny - 1)(row)
            else:
                row()

    def signal(semaphore, partner):
        pl.semaphore_signal(semaphore, inc=1, device_id=partner, device_id_type=MESH)

    loads = [
        pltpu.make_async_copy(c_hbm.at[:, 0, 0:8], stage.at[0:SPECIES], local_sem.at[0]),
        pltpu.make_async_copy(m_hbm.at[0, 0:8], stage.at[TORT], local_sem.at[1]),
        pltpu.make_async_copy(d_hbm.at[0, 0:8], stage.at[DIRE], local_sem.at[2]),
        pltpu.make_async_copy(soil_hbm, soil_v, local_sem.at[3]),
        pltpu.make_async_copy(mix_hbm, mix_ref, local_sem.at[4]),
        pltpu.make_async_copy(pair_hbm, pair_ref, local_sem.at[5]),
        pltpu.make_async_copy(obs_hbm, obs_v, local_sem.at[6]),
    ]
    rim[...] = jnp.zeros_like(rim)
    rim_y[...] = jnp.zeros_like(rim_y)
    barrier = pltpu.get_barrier_semaphore()
    neighbours(lambda dx, dy, _: signal(barrier, (x + dx, y + dy)))
    for copy in loads:
        copy.start()
    group_a = []
    for i in range(1, 16):
        core, mid, high = i % 2, (i // 2) % 4, i // 8
        group_a.append((x_hi * 8 + (x_mid + mid) % 4 * 2 + (x_core + core) % 2, (y_hi + high) % 2 * 4 + y_lo))
    group_b = []
    for i in range(1, 16):
        group_b.append(((x_hi + i // 4) % 4 * 8 + x_mid * 2 + x_core, y_hi * 4 + (y_lo + i % 4) % 4))
    direct = jnp.logical_and(y_hi == 0, x_mid < 2)
    for partner in group_a + group_b:
        signal(barrier, partner)
    arrivals = len(group_a + group_b)
    for dx, dy, _ in offsets():
        there = in_x[dx]
        if dy:
            there = jnp.logical_and(there, y > 0 if dy < 0 else y < ny - 1)
        arrivals = arrivals + there.astype(jnp.int32)

    stage[SOIL] = jnp.zeros((8, LANES), jnp.float32)
    stage[SOIL + 1] = jnp.zeros((8, LANES), jnp.float32)
    for copy in loads[:4]:
        copy.wait()
    stage[SOIL, 0:1] = soil_v[...].astype(jnp.float32)
    flat = stage.reshape((ROWS + 1) * 8, LANES)
    for z in range(STEPS + 1):
        for half in range(2):
            block[pl.ds(z * ROWS + half * 8, 8)] = flat[pl.ds(half * 64 + z, 8, stride=8)]
    strip[0], strip[1] = fold_strips(pack_strips([block[i * 8 : i * 8 + 8] for i in range(2 * STEPS)]))

    pl.semaphore_wait(barrier, arrivals)

    @pl.when(direct)
    def _():
        for partner in group_a:
            signal(ready, partner)


    def copy_of(src, dst, sems, number, partner):
        return pltpu.make_async_remote_copy(
            src_ref=src, dst_ref=dst, send_sem=send_sem.at[sems + number], recv_sem=recv_sem.at[sems + number],
            device_id=partner, device_id_type=MESH,
        )

    def halo_copy(dx, dy, depths):
        if dy:
            src, dst = strip.at[(1 - dy) // 2], halo_y.at[STRIP[-dx, -dy]]
        else:
            src, dst = block.at[pl.ds(0, depths * ROWS)], halo.at[pl.ds(HALO[-dx], depths * ROWS)]
        return copy_of(src, dst, 0, SEM[-dx, -dy], (x + dx, y + dy))

    def rim_copy(dx, dy, _):
        if dy:
            src, dst = rim_strip.at[(1 - dy) // 2], rim_y.at[STRIP[-dx, -dy]]
        else:
            src, dst = rim_out, rim.at[pl.ds(RIM[-dx], RIM_ROWS)]
        return copy_of(src, dst, len(SEM), SEM[-dx, -dy], (x + dx, y + dy))

    def part_copy(index, dst, partner):
        return copy_of(part_out.at[index % 2], dst, 2 * len(SEM), index, partner)

    neighbours(lambda *place: halo_copy(*place).start(), (1, -1))

    def along(places):
        @pl.when(all_in_x)
        def _():
            for place in places:
                halo_copy(*place).start()

        @pl.when(jnp.logical_not(all_in_x))
        def _():
            for place in places:
                pl.when(in_x[place[0]])(lambda place=place: halo_copy(*place).start())

    pl.when(x % 8 < 4)(lambda: along(ALONG_X))
    pl.when(x % 8 >= 4)(lambda: along(ALONG_X[::-1]))

    for copy in loads[4:]:
        copy.wait()
    square[...] = jnp.zeros((LANES, LANES), jnp.float32)
    diagonal = lax.broadcasted_iota(jnp.int32, (SPECIES, SPECIES), 0) == lax.broadcasted_iota(
        jnp.int32, (SPECIES, SPECIES), 1
    )
    pair = pair_ref[...].astype(jnp.float32)
    for level in range(LAYERS):
        entry = mix_ref[:, level, :]
        square[level * ROWS : level * ROWS + SPECIES, 0:SPECIES] = jnp.where(diagonal, entry, entry * pair)
    plain = square[...]
    turned = plain.T
    for level in range(LAYERS):
        for t in range(SPECIES):
            for half in range(2):
                row = level * ROWS + half * 8
                fwd_parts[level, t, half] = jnp.broadcast_to(plain[row : row + 8, t : t + 1], (8, LANES))
                col = level * ROWS + t
                adj_parts[level, t, half] = jnp.broadcast_to(
                    turned[half * 8 : half * 8 + 8, col : col + 1], (8, LANES)
                )

    def arrived(copy, rows=(-1, 1, 0)):
        def act(dx, dy, depths):
            copy(-dx, -dy, depths).wait_recv()
        neighbours(act, rows)

    species_row = lax.broadcasted_iota(jnp.int32, (1, 2, 8, LANES), 1) * 8 + lax.broadcasted_iota(
        jnp.int32, (1, 2, 8, LANES), 2
    )
    right_half = lane((8, LANES)) < LANES // 2
    in_y = jnp.where(right_half, y + 1, y - 1)
    in_y = jnp.logical_and(in_y >= 0, in_y < ny)

    def cells(ref, start, depths):
        return ref[pl.ds(start, depths * ROWS)].reshape(depths, 2, 8, LANES)

    def row_of(value, row):
        depths = value.shape[0]
        return jnp.broadcast_to(value[:, row // 8, row % 8 : row % 8 + 1, :], (depths, 8, LANES))

    def zero_unless(valid, value):
        return jnp.where(jnp.broadcast_to(valid, value.shape), value, 0.0)

    def unpack(value, valid):
        depths = value.shape[0]
        state = jnp.where(jnp.broadcast_to(species_row < SPECIES, value.shape), value, 0.0)
        tort, dire = row_of(value, TORT), row_of(value, DIRE)
        soil = row_of(value[:1], SOIL)[0]
        if valid is not None:
            state = zero_unless(valid, state)
            tort, dire = zero_unless(valid, tort), zero_unless(valid, dire)
            soil = jnp.where(valid, soil, -1.0)
        weight = (0.5 * DT) * jnp.exp(tort)
        turn = weight * dire
        shape = (depths, 1, 8, LANES)
        return state, weight.reshape(shape), turn.reshape(shape), dire.reshape(shape), soil

    main, edge = {}, {}
    weight_m, weight_e, turn_m, turn_e, soil_m, soil_e = {}, {}, {}, {}, {}, {}
    main[0], weight_m[0], turn_m[0], own_dire, soil_m[0] = unpack(cells(block, 0, STEPS + 1), None)
    select_table(fwd, FWD_MAIN[0], fwd_parts, soil_m[0])

    arrived(halo_copy, (-1, 1))
    for dx in range(1 - STEPS, STEPS):
        depths = STEPS - abs(dx)
        left, right = unfold_strips(halo_y[STRIP[dx, -1]], halo_y[STRIP[dx, 1]])
        raw = jnp.stack([unpack_strip(left, right, i) for i in range(2 * depths)])
        valid = jnp.logical_and(in_y, jnp.broadcast_to(in_x[dx], (8, LANES)))
        edge[dx], weight_e[dx], turn_e[dx], _, soil_e[dx] = unpack(raw.reshape(depths, 2, 8, LANES), valid)
    for dx, column in FWD_EDGE.items():
        select_table(fwd, column, fwd_parts, soil_e[dx])

    arrived(halo_copy, (0,))
    for dx, _, depths in ALONG_X:
        valid = jnp.broadcast_to(in_x[dx], (8, LANES))
        main[dx], weight_m[dx], turn_m[dx], _, soil_m[dx] = unpack(cells(halo, HALO[dx], depths), valid)
    main, weight_m, turn_m = ({dx: field[dx] for dx in sorted(field)} for field in (main, weight_m, turn_m))
    for dx, column in FWD_MAIN.items():
        if dx:
            select_table(fwd, column, fwd_parts, soil_m[dx])

    def face_sums(main_w, edge_w, outside):
        out = {}
        for kind, field in (("m", main_w), ("e", edge_w)):
            for dx in field:
                value = field[dx]
                if dx + 1 in field:
                    n = min(value.shape[0], field[dx + 1].shape[0])
                    out["x" + kind, dx] = field[dx + 1][:n] + value[:n]
                parts = [value[:1] + outside]
                if value.shape[0] > 1:
                    parts.append(value[1:] + value[:-1])
                out["z" + kind, dx] = jnp.concatenate(parts, 0) if len(parts) > 1 else parts[0]
        for dx in edge_w:
            n = edge_w[dx].shape[0]
            a, b = y_next(main_w[dx][:n], edge_w[dx][:n])
            out["ym", dx] = a + main_w[dx][:n]
            out["ye", dx] = b + edge_w[dx][:n]
        return out

    coeff = face_sums(weight_m, weight_e, 0.5 * DT)
    slope = face_sums(turn_m, turn_e, 0.0)

    diffs, diffs_dot = [], []
    main_dot, edge_dot = None, None
    for k in range(STEPS):
        reach = STEPS - 1 - k
        diff = faces(main, edge, False)
        diffs.append(diff)
        flux = times(coeff, diff)
        flux_dot = times(slope, diff)
        if main_dot is not None:
            diff_dot = faces(main_dot, edge_dot, False)
            flux_dot = plus(flux_dot, times(coeff, diff_dot))
        else:
            diff_dot = None
        diffs_dot.append(diff_dot)
        spread_m, spread_e = gathered(flux, reach, False)
        dot_m, dot_e = gathered(flux_dot, reach, False)
        new = [{}, {}, {}, {}]
        for kind, table, old, old_dot, spread, dot in (
            (0, FWD_MAIN, main, main_dot, spread_m, dot_m),
            (1, FWD_EDGE, edge, edge_dot, spread_e, dot_e),
        ):
            for dx in spread:
                n = spread[dx].shape[0]
                new[kind][dx] = old[dx][:n] + mixed(fwd, table[dx], spread[dx])
                moved = mixed(fwd, table[dx], dot[dx])
                new[2 + kind][dx] = moved if old_dot is None else old_dot[dx][:n] + moved
        main, edge, main_dot, edge_dot = new

    obs = jnp.concatenate([obs_v[s] for s in range(SPECIES)] + [jnp.zeros((ROWS - SPECIES, LANES), jnp.float32)], 0)
    miss = main[0].reshape(ROWS, LANES) - obs
    miss_dot = main_dot[0].reshape(ROWS, LANES)
    square_sum = jnp.sum(miss * miss, 0, keepdims=True)
    cross_sum = jnp.sum(miss * miss_dot, 0, keepdims=True)
    front = lane((1, LANES)) < LANES // 2
    half_row = LANES // 2
    part = jnp.where(front, square_sum + spin(square_sum, half_row), cross_sum + spin(cross_sum, half_row))
    part_out[0] = part
    pl.semaphore_wait(ready, 4 - direct.astype(jnp.int32))

    def straight(across, mid):
        north, east = across // 4, across % 4
        offset = (north - x_hi + 4) % 4 * 4 + (east - y_lo + 4) % 4

        @pl.when(offset > 0)
        def _():
            for core in (1, 0):
                step = (core + x_core) % 2 + (mid - x_mid + 4) % 4 * 2 + y_hi * 8
                partner = north * 8 + mid * 2 + core, jnp.int32(east)
                part_copy(2, part_all.at[offset * 16 - 1 + step], partner).start()

    def along_z(height):
        high, mid = height // 4, height % 4
        for core in (1, 0):
            step = (core + x_core) % 2 + (mid - x_mid + 4) % 4 * 2 + (high + y_hi) % 2 * 8

            @pl.when(step > 0)
            def _(core=core, step=step):
                partner = x_hi * 8 + mid * 2 + core, high * 4 + y_lo
                part_copy(0, part_all.at[step - 1], partner).start()

    straight(0, 0)
    for across in range(4):
        straight(across, 1)
    for height in range(8):
        along_z(height)
    for across in range(1, 16):
        straight(across, 0)
    for across in range(4, 16):
        straight(across, 1)

    shared = miss[8:] + pltpu.roll(miss_dot[8:], 4, 0)
    tiles = [miss[:8], miss_dot[:8], shared]
    for i, tile in enumerate(tiles):
        rim_out[i * 8 : i * 8 + 8] = tile
    rim_strip[0], rim_strip[1] = fold_strips(pack_strips(tiles))
    neighbours(lambda *place: rim_copy(*place).start())

    for dx, column in ADJ_MAIN.items():
        select_table(adj, column, adj_parts, soil_m[dx])
    for dx, column in ADJ_EDGE.items():
        select_table(adj, column, adj_parts, soil_e[dx])

    near, far = part_all.at[pl.ds(0, 15)], part_all.at[pl.ds(15, 240)]

    def all_arrived(buffer, index):
        pltpu.make_async_copy(buffer, buffer, recv_sem.at[2 * len(SEM) + index]).wait()

    @pl.when(jnp.logical_not(direct))
    def _():
        all_arrived(near, 0)
        part_out[1] = part + jnp.sum(part_all[0:15], 0)
        for slot, partner in enumerate(group_b):
            part_copy(1, part_b.at[slot], partner).start()

    arrived(rim_copy)
    lam_m, lam_e, mu_m, mu_e = {}, {}, {}, {}

    def rim_fields(tiles):
        fields = jnp.stack([tiles[0], tiles[2], tiles[1], pltpu.roll(tiles[2], 4, 0)])
        fields = fields.reshape(2, 2, 8, LANES)
        return fields[:1], fields[1:]

    for dx in range(-STEPS, STEPS + 1):
        own = [rim[pl.ds(RIM[dx] + i * 8, 8)] for i in range(3)] if dx else tiles
        lam_m[dx], mu_m[dx] = rim_fields(own)
        if abs(dx) < STEPS:
            left, right = unfold_strips(rim_y[STRIP[dx, -1]], rim_y[STRIP[dx, 1]])
            lam_e[dx], mu_e[dx] = rim_fields([unpack_strip(left, right, i) for i in range(3)])

    sums = {}

    def into(key, value):
        value = value[:, 0] + value[:, 1]
        if key in sums:
            old = sums[key]
            n = old.shape[0]
            sums[key] = jnp.concatenate([old + value[:n], value[n:]], 0) if value.shape[0] > n else old + value
        else:
            sums[key] = value

    own = (("xm", 0), ("xm", -1), ("zm", 0), ("ym", 0), ("ye", 0))
    for k in reversed(range(STEPS)):
        reach = STEPS - 1 - k
        u_m = {dx: mixed(adj, ADJ_MAIN[dx], lam_m[dx]) for dx in lam_m}
        v_m = {dx: mixed(adj, ADJ_MAIN[dx], mu_m[dx]) for dx in mu_m}
        u_e = {dx: mixed(adj, ADJ_EDGE[dx], lam_e[dx]) for dx in lam_e}
        v_e = {dx: mixed(adj, ADJ_EDGE[dx], mu_e[dx]) for dx in mu_e}
        diff_u, diff_v = faces(u_m, u_e, True), faces(v_m, v_e, True)
        for key in own:
            du, dv, dc = diff_u[key], diff_v[key], diffs[k][key][: diff_u[key].shape[0]]
            into(("g", key), du * dc)
            second = dv * dc
            if diffs_dot[k] is not None:
                second = second + du * diffs_dot[k][key][: du.shape[0]]
            into(("h", key), second)
        if k == 0:
            break
        need = lambda diff: {
            key: value for key, value in diff.items()
            if key[0][0] == "x" or abs(key[1]) <= (k if key[0] != "ze" else k - 1)
        }
        diff_u, diff_v = need(diff_u), need(diff_v)
        step_m, step_e = gathered(times(coeff, diff_u), k, True)
        dot_m, dot_e = gathered(plus(times(coeff, diff_v), times(slope, diff_u)), k, True)

        def added(old, step):
            n = old.shape[0]
            return jnp.concatenate([old + step[:n], step[n:]], 0)

        lam_m, lam_e = (
            {dx: added(lam_m[dx], step_m[dx]) for dx in step_m},
            {dx: added(lam_e[dx], step_e[dx]) for dx in step_e},
        )
        mu_m, mu_e = (
            {dx: added(mu_m[dx], dot_m[dx]) for dx in dot_m},
            {dx: added(mu_e[dx], dot_e[dx]) for dx in dot_e},
        )

    def per_cell(name):
        y_sum = sums[name, ("ym", 0)]
        side = sums[name, ("xm", 0)] + sums[name, ("xm", -1)] + y_sum
        side = side + y_prev(y_sum, sums[name, ("ye", 0)])[0]
        depth = sums[name, ("zm", 0)]
        n = side.shape[0]
        total = jnp.concatenate([side + depth[:n] + depth[1:], depth[n:]], 0)
        return jnp.sum(total, 1, keepdims=True)

    weight = weight_m[0][:, 0, :1, :]
    plain_part = -weight * per_cell("g")
    dot_part = -weight * per_cell("h") + own_dire[:, 0, :1, :] * plain_part

    neighbours(lambda *place: halo_copy(*place).wait_send())
    neighbours(lambda *place: rim_copy(*place).wait_send())
    def all_sent(buffer, index):
        pltpu.make_async_copy(buffer, buffer, send_sem.at[2 * len(SEM) + index]).wait()

    all_sent(near, 0)
    all_sent(part_all.at[pl.ds(0, 60)], 2)

    @pl.when(direct)
    def _():
        all_arrived(near, 0)
        all_arrived(far, 2)
        rest = part_all[...].reshape(17, 15, 1, LANES)
        part_sum[...] = part_out[0] + jnp.sum(jnp.sum(rest, 0), 0)

    @pl.when(jnp.logical_not(direct))
    def _():
        all_sent(part_b, 1)
        all_arrived(part_b, 1)
        part_sum[...] = part_out[1] + jnp.sum(part_b[...], 0)

    part = part_sum[...]
    total = jnp.sum(jnp.where(front, part, 0.0), 1, keepdims=True)
    cross = jnp.sum(jnp.where(front, 0.0, part), 1, keepdims=True)
    count = float(SPECIES * nx * ny * LANES)
    factor = count / total
    second = -2.0 * count * cross / (total * total)
    zero = jnp.zeros((1, LANES), jnp.float32)
    for z in range(16):
        one, two = (dot_part[z], plain_part[z]) if z <= STEPS else (zero, zero)
        out_ref[0, z : z + 1, :] = factor * one + second * two


def solution(mesh):
    nx, ny = mesh.shape["gx"], mesh.shape["gy"]

    def body(c_start, log_tort, direction, mix_inverse, pair_mask, soil_layer, observed):
        f32 = jnp.float32
        hbm = pl.BlockSpec(memory_space=pltpu.HBM)
        vmem = pl.BlockSpec(memory_space=pltpu.VMEM)
        return pl.pallas_call(
            lambda *refs: kernel(nx, ny, *refs),
            out_shape=jax.ShapeDtypeStruct((1, 16, LANES), f32),
            in_specs=[hbm] * 7,
            out_specs=vmem,
            scratch_shapes=[
                pltpu.VMEM((ROWS + 1, 8, LANES), f32),
                pltpu.VMEM((1, LANES), jnp.int32),
                pltpu.VMEM((SPECIES, 1, LANES), f32),
                pltpu.VMEM((SPECIES, LAYERS, SPECIES), f32),
                pltpu.VMEM((SPECIES, SPECIES), jnp.int32),
                pltpu.VMEM(((STEPS + 1) * ROWS, LANES), f32),
                pltpu.VMEM((2, 4, LANES), f32),
                pltpu.VMEM((HALO_ROWS, LANES), f32),
                pltpu.VMEM((len(ACROSS), 4, LANES), f32),
                pltpu.VMEM((RIM_ROWS, LANES), f32),
                pltpu.VMEM((2, 4, LANES), f32),
                pltpu.VMEM((len(ALONG_X) * RIM_ROWS, LANES), f32),
                pltpu.VMEM((len(ACROSS), 4, LANES), f32),
                pltpu.VMEM((2, 1, LANES), f32),
                pltpu.VMEM((255, 1, LANES), f32),
                pltpu.VMEM((15, 1, LANES), f32),
                pltpu.VMEM((1, LANES), f32),
                pltpu.VMEM((LANES, LANES), f32),
                pltpu.VMEM((LAYERS, SPECIES, 2, 8, LANES), f32),
                pltpu.VMEM((LAYERS, SPECIES, 2, 8, LANES), f32),
                pltpu.VMEM((8, SPECIES, 2, 8, LANES), f32),
                pltpu.VMEM((12, SPECIES, 2, 8, LANES), f32),
                pltpu.SemaphoreType.DMA((7,)),
                pltpu.SemaphoreType.DMA((2 * len(SEM) + 3,)),
                pltpu.SemaphoreType.DMA((2 * len(SEM) + 3,)),
                pltpu.SemaphoreType.REGULAR,
            ],
            compiler_params=pltpu.CompilerParams(
                collective_id=0, has_side_effects=True, vmem_limit_bytes=32 * 1024 * 1024
            ),
        )(*(
            pltpu.with_memory_space_constraint(value, pltpu.HBM)
            for value in (
                c_start, log_tort, direction, mix_inverse.transpose(1, 0, 2), pair_mask, soil_layer, observed,
            )
        ))

    return jax.shard_map(
        body,
        mesh=mesh,
        in_specs=(
            P(None, "gx", None, "gy"),
            P("gx", None, "gy"),
            P("gx", None, "gy"),
            P(),
            P(),
            P("gx", "gy"),
            P(None, "gx", "gy"),
        ),
        out_specs=P("gx", None, "gy"),
        check_vma=False,
    )
```

```python
import jax
import jax.numpy as jnp
from jax import lax
from jax.experimental import pallas as pl
from jax.experimental.pallas import tpu as pltpu
from jax.sharding import PartitionSpec as P

MESH = pl.DeviceIdType.MESH
DT = 0.04
STEPS = 3
SPECIES = 12
LAYERS = 4
LANES = 128
ROWS = 16
TORT, DIRE, SOIL = 12, 13, 14


def offsets():
    found = []
    for dx in range(-STEPS, STEPS + 1):
        for dy in (-1, 0, 1):
            depths = STEPS + 1 - abs(dx) - (1 if dy else 0)
            if depths > 0 and (dx or dy):
                found.append((dx, dy, depths))
    return found


ALONG_X = [(dx, dy, depths) for dx, dy, depths in offsets() if dy == 0]
ACROSS = [(dx, dy) for dx, dy, _ in offsets() if dy]
STRIP = {place: i for i, place in enumerate(ACROSS)}
SEM = {(dx, dy): i for i, (dx, dy, _) in enumerate(offsets())}
HALO, HALO_ROWS = {}, 0
for dx, _, depths in ALONG_X:
    HALO[dx] = HALO_ROWS
    HALO_ROWS += depths * ROWS
RIM_ROWS = 24
RIM = {dx: i * RIM_ROWS for i, (dx, _, _) in enumerate(ALONG_X)}
FWD_MAIN = {dx: i for i, dx in enumerate(range(-2, 3))}
FWD_EDGE = {dx: 5 + i for i, dx in enumerate(range(-1, 2))}
ADJ_MAIN = {dx: i for i, dx in enumerate(range(-3, 4))}
ADJ_EDGE = {dx: 7 + i for i, dx in enumerate(range(-2, 3))}


def lane(shape):
    return lax.broadcasted_iota(jnp.int32, shape, len(shape) - 1)


def spin(value, by):
    return pltpu.roll(value, by % LANES, value.ndim - 1)


def y_next(main, edge):
    last = lane(main.shape) == LANES - 1
    a, b = spin(main, -1), spin(edge, -1)
    return jnp.where(last, b, a), jnp.where(last, a, b)


def y_prev(main, edge):
    first = lane(main.shape) == 0
    a, b = spin(main, 1), spin(edge, 1)
    return jnp.where(first, b, a), jnp.where(first, a, b)


def pack_strips(tiles):
    group = lane((8, LANES)) // 8
    packed = tiles[0]
    for i, tile in enumerate(tiles[1:], 1):
        packed = jnp.where(group == i, spin(tile, 8 * i), packed)
        packed = jnp.where(group == 15 - i, spin(tile, -8 * i), packed)
    return packed


FOLD = 48


def fold_strips(packed):
    place = lane((8, LANES))
    last = jnp.where(place >= LANES - FOLD, packed, pltpu.roll(spin(packed, -FOLD), 4, 0))
    first = jnp.where(place < FOLD, packed, pltpu.roll(spin(packed, FOLD), 4, 0))
    return last[:4], first[:4]


def unfold_strips(left, right):
    return jnp.concatenate([left, spin(left, FOLD)], 0), jnp.concatenate([right, spin(right, -FOLD)], 0)


def unpack_strip(left, right, i):
    return jnp.where(lane((8, LANES)) < LANES // 2, spin(right, -8 * i), spin(left, 8 * i))


def faces(main, edge, closed):
    out = {}
    for kind, field in (("m", main), ("e", edge)):
        for dx in field:
            value = field[dx]
            if dx + 1 in field:
                n = min(value.shape[0], field[dx + 1].shape[0])
                out["x" + kind, dx] = field[dx + 1][:n] - value[:n]
            parts = [value[:1]]
            if value.shape[0] > 1:
                parts.append(value[1:] - value[:-1])
            if closed:
                parts.append(-value[-1:])
            out["z" + kind, dx] = jnp.concatenate(parts, 0) if len(parts) > 1 else parts[0]
    for dx in edge:
        n = edge[dx].shape[0]
        a, b = y_next(main[dx][:n], edge[dx][:n])
        out["ym", dx] = a - main[dx][:n]
        out["ye", dx] = b - edge[dx][:n]
    return out


def times(coeff, diff):
    return {key: coeff[key][: diff[key].shape[0]] * diff[key] for key in diff}


def plus(one, two):
    return {key: one[key] + two[key] for key in one}


def gathered(flux, reach, closed):
    result = []
    for kind, most in (("m", reach), ("e", reach - 1)):
        field = {}
        for dx in range(-most, most + 1):
            depth = flux["z" + kind, dx]
            n = depth.shape[0] - 1
            total = depth[1:] - depth[:-1]
            a, b = y_prev(flux["ym", dx], flux["ye", dx])
            back = a if kind == "m" else b
            side = (
                flux["x" + kind, dx][:n]
                - flux["x" + kind, dx - 1][:n]
                + flux["y" + kind, dx][:n]
                - back[:n]
            )
            if closed:
                total = jnp.concatenate([total[:n] + side, -depth[n:]], 0)
            else:
                total = total + side
            field[dx] = total
        result.append(field)
    return result


def mixed(table, column, value):
    total = None
    for t in range(SPECIES):
        part = table[column, t] * value[:, t // 8 : t // 8 + 1, t % 8 : t % 8 + 1, :]
        total = part if total is None else total + part
    return total


def select_table(table, column, parts, soil):
    masks = [soil == float(level) for level in range(LAYERS)]
    for t in range(SPECIES):
        for half in range(2):
            value = jnp.zeros((8, LANES), jnp.float32)
            for level in range(LAYERS):
                value = jnp.where(masks[level], parts[level, t, half], value)
            table[column, t, half] = value


def kernel(
    nx, ny, c_hbm, m_hbm, d_hbm, mix_hbm, pair_hbm, soil_hbm, obs_hbm, out_ref,
    stage, soil_v, obs_v, mix_ref, pair_ref, block, strip, halo, halo_y, rim_out, rim_strip, rim, rim_y,
    part_out, part_all, part_b, part_sum,
    square, fwd_parts, adj_parts, fwd, adj,
    local_sem, send_sem, recv_sem, ready,
):
    x, y = lax.axis_index("gx"), lax.axis_index("gy")
    x_hi, x_mid, x_core = x // 8, (x // 2) % 4, x % 2
    y_hi, y_lo = y // 4, y % 4

    in_x = {dx: jnp.logical_and(x + dx >= 0, x + dx < nx) for dx in range(-STEPS, STEPS + 1)}
    all_in_x = jnp.logical_and(x >= STEPS, x < nx - STEPS)

    def neighbours(act, rows=(-1, 1, 0)):
        for dy in rows:
            places = [place for place in offsets() if place[1] == dy]

            def row(places=places):
                @pl.when(all_in_x)
                def _():
                    for place in places:
                        act(*place)

                @pl.when(jnp.logical_not(all_in_x))
                def _():
                    for place in places:
                        pl.when(in_x[place[0]])(lambda place=place: act(*place))

            if dy:
                pl.when(y > 0 if dy < 0 else y < ny - 1)(row)
            else:
                row()

    def signal(semaphore, partner):
        pl.semaphore_signal(semaphore, inc=1, device_id=partner, device_id_type=MESH)

    loads = [
        pltpu.make_async_copy(c_hbm.at[:, 0, 0:8], stage.at[0:SPECIES], local_sem.at[0]),
        pltpu.make_async_copy(m_hbm.at[0, 0:8], stage.at[TORT], local_sem.at[1]),
        pltpu.make_async_copy(d_hbm.at[0, 0:8], stage.at[DIRE], local_sem.at[2]),
        pltpu.make_async_copy(soil_hbm, soil_v, local_sem.at[3]),
        pltpu.make_async_copy(mix_hbm, mix_ref, local_sem.at[4]),
        pltpu.make_async_copy(pair_hbm, pair_ref, local_sem.at[5]),
        pltpu.make_async_copy(obs_hbm, obs_v, local_sem.at[6]),
    ]
    rim[...] = jnp.zeros_like(rim)
    rim_y[...] = jnp.zeros_like(rim_y)
    barrier = pltpu.get_barrier_semaphore()
    neighbours(lambda dx, dy, _: signal(barrier, (x + dx, y + dy)))
    for copy in loads:
        copy.start()
    group_a = []
    for i in range(1, 16):
        core, mid, high = i % 2, (i // 2) % 4, i // 8
        group_a.append((x_hi * 8 + (x_mid + mid) % 4 * 2 + (x_core + core) % 2, (y_hi + high) % 2 * 4 + y_lo))
    group_b = []
    for i in range(1, 16):
        group_b.append(((x_hi + i // 4) % 4 * 8 + x_mid * 2 + x_core, y_hi * 4 + (y_lo + i % 4) % 4))
    direct = jnp.logical_and(y_hi == 0, x_mid < 2)
    for partner in group_a + group_b:
        signal(barrier, partner)
    arrivals = len(group_a + group_b)
    for dx, dy, _ in offsets():
        there = in_x[dx]
        if dy:
            there = jnp.logical_and(there, y > 0 if dy < 0 else y < ny - 1)
        arrivals = arrivals + there.astype(jnp.int32)

    stage[SOIL] = jnp.zeros((8, LANES), jnp.float32)
    stage[SOIL + 1] = jnp.zeros((8, LANES), jnp.float32)
    for copy in loads[:4]:
        copy.wait()
    stage[SOIL, 0:1] = soil_v[...].astype(jnp.float32)
    flat = stage.reshape((ROWS + 1) * 8, LANES)
    for z in range(STEPS + 1):
        for half in range(2):
            block[pl.ds(z * ROWS + half * 8, 8)] = flat[pl.ds(half * 64 + z, 8, stride=8)]
    strip[0], strip[1] = fold_strips(pack_strips([block[i * 8 : i * 8 + 8] for i in range(2 * STEPS)]))

    pl.semaphore_wait(barrier, arrivals)

    @pl.when(direct)
    def _():
        for partner in group_a:
            signal(ready, partner)


    def copy_of(src, dst, sems, number, partner):
        return pltpu.make_async_remote_copy(
            src_ref=src, dst_ref=dst, send_sem=send_sem.at[sems + number], recv_sem=recv_sem.at[sems + number],
            device_id=partner, device_id_type=MESH,
        )

    def halo_copy(dx, dy, depths):
        if dy:
            src, dst = strip.at[(1 - dy) // 2], halo_y.at[STRIP[-dx, -dy]]
        else:
            src, dst = block.at[pl.ds(0, depths * ROWS)], halo.at[pl.ds(HALO[-dx], depths * ROWS)]
        return copy_of(src, dst, 0, SEM[-dx, -dy], (x + dx, y + dy))

    def rim_copy(dx, dy, _):
        if dy:
            src, dst = rim_strip.at[(1 - dy) // 2], rim_y.at[STRIP[-dx, -dy]]
        else:
            src, dst = rim_out, rim.at[pl.ds(RIM[-dx], RIM_ROWS)]
        return copy_of(src, dst, len(SEM), SEM[-dx, -dy], (x + dx, y + dy))

    def part_copy(index, dst, partner):
        return copy_of(part_out.at[index % 2], dst, 2 * len(SEM), index, partner)

    neighbours(lambda *place: halo_copy(*place).start(), (1, -1))

    def along(places):
        @pl.when(all_in_x)
        def _():
            for place in places:
                halo_copy(*place).start()

        @pl.when(jnp.logical_not(all_in_x))
        def _():
            for place in places:
                pl.when(in_x[place[0]])(lambda place=place: halo_copy(*place).start())

    pl.when(x % 8 < 4)(lambda: along(ALONG_X))
    pl.when(x % 8 >= 4)(lambda: along(ALONG_X[::-1]))

    for copy in loads[4:]:
        copy.wait()
    square[...] = jnp.zeros((LANES, LANES), jnp.float32)
    diagonal = lax.broadcasted_iota(jnp.int32, (SPECIES, SPECIES), 0) == lax.broadcasted_iota(
        jnp.int32, (SPECIES, SPECIES), 1
    )
    pair = pair_ref[...].astype(jnp.float32)
    for level in range(LAYERS):
        entry = mix_ref[:, level, :]
        square[level * ROWS : level * ROWS + SPECIES, 0:SPECIES] = jnp.where(diagonal, entry, entry * pair)
    plain = square[...]
    turned = plain.T
    for level in range(LAYERS):
        for t in range(SPECIES):
            for half in range(2):
                row = level * ROWS + half * 8
                fwd_parts[level, t, half] = jnp.broadcast_to(plain[row : row + 8, t : t + 1], (8, LANES))
                col = level * ROWS + t
                adj_parts[level, t, half] = jnp.broadcast_to(
                    turned[half * 8 : half * 8 + 8, col : col + 1], (8, LANES)
                )

    def arrived(copy, rows=(-1, 1, 0)):
        def act(dx, dy, depths):
            copy(-dx, -dy, depths).wait_recv()
        neighbours(act, rows)

    species_row = lax.broadcasted_iota(jnp.int32, (1, 2, 8, LANES), 1) * 8 + lax.broadcasted_iota(
        jnp.int32, (1, 2, 8, LANES), 2
    )
    right_half = lane((8, LANES)) < LANES // 2
    in_y = jnp.where(right_half, y + 1, y - 1)
    in_y = jnp.logical_and(in_y >= 0, in_y < ny)

    def cells(ref, start, depths):
        return ref[pl.ds(start, depths * ROWS)].reshape(depths, 2, 8, LANES)

    def row_of(value, row):
        depths = value.shape[0]
        return jnp.broadcast_to(value[:, row // 8, row % 8 : row % 8 + 1, :], (depths, 8, LANES))

    def zero_unless(valid, value):
        return jnp.where(jnp.broadcast_to(valid, value.shape), value, 0.0)

    def unpack(value, valid):
        depths = value.shape[0]
        state = jnp.where(jnp.broadcast_to(species_row < SPECIES, value.shape), value, 0.0)
        tort, dire = row_of(value, TORT), row_of(value, DIRE)
        soil = row_of(value[:1], SOIL)[0]
        if valid is not None:
            state = zero_unless(valid, state)
            tort, dire = zero_unless(valid, tort), zero_unless(valid, dire)
            soil = jnp.where(valid, soil, -1.0)
        weight = (0.5 * DT) * jnp.exp(tort)
        turn = weight * dire
        shape = (depths, 1, 8, LANES)
        return state, weight.reshape(shape), turn.reshape(shape), dire.reshape(shape), soil

    main, edge = {}, {}
    weight_m, weight_e, turn_m, turn_e, soil_m, soil_e = {}, {}, {}, {}, {}, {}
    main[0], weight_m[0], turn_m[0], own_dire, soil_m[0] = unpack(cells(block, 0, STEPS + 1), None)
    select_table(fwd, FWD_MAIN[0], fwd_parts, soil_m[0])

    arrived(halo_copy, (-1, 1))
    for dx in range(1 - STEPS, STEPS):
        depths = STEPS - abs(dx)
        left, right = unfold_strips(halo_y[STRIP[dx, -1]], halo_y[STRIP[dx, 1]])
        raw = jnp.stack([unpack_strip(left, right, i) for i in range(2 * depths)])
        valid = jnp.logical_and(in_y, jnp.broadcast_to(in_x[dx], (8, LANES)))
        edge[dx], weight_e[dx], turn_e[dx], _, soil_e[dx] = unpack(raw.reshape(depths, 2, 8, LANES), valid)
    for dx, column in FWD_EDGE.items():
        select_table(fwd, column, fwd_parts, soil_e[dx])

    arrived(halo_copy, (0,))
    for dx, _, depths in ALONG_X:
        valid = jnp.broadcast_to(in_x[dx], (8, LANES))
        main[dx], weight_m[dx], turn_m[dx], _, soil_m[dx] = unpack(cells(halo, HALO[dx], depths), valid)
    main, weight_m, turn_m = ({dx: field[dx] for dx in sorted(field)} for field in (main, weight_m, turn_m))
    for dx, column in FWD_MAIN.items():
        if dx:
            select_table(fwd, column, fwd_parts, soil_m[dx])

    def face_sums(main_w, edge_w, outside):
        out = {}
        for kind, field in (("m", main_w), ("e", edge_w)):
            for dx in field:
                value = field[dx]
                if dx + 1 in field:
                    n = min(value.shape[0], field[dx + 1].shape[0])
                    out["x" + kind, dx] = field[dx + 1][:n] + value[:n]
                parts = [value[:1] + outside]
                if value.shape[0] > 1:
                    parts.append(value[1:] + value[:-1])
                out["z" + kind, dx] = jnp.concatenate(parts, 0) if len(parts) > 1 else parts[0]
        for dx in edge_w:
            n = edge_w[dx].shape[0]
            a, b = y_next(main_w[dx][:n], edge_w[dx][:n])
            out["ym", dx] = a + main_w[dx][:n]
            out["ye", dx] = b + edge_w[dx][:n]
        return out

    coeff = face_sums(weight_m, weight_e, 0.5 * DT)
    slope = face_sums(turn_m, turn_e, 0.0)

    diffs, diffs_dot = [], []
    main_dot, edge_dot = None, None
    for k in range(STEPS):
        reach = STEPS - 1 - k
        diff = faces(main, edge, False)
        diffs.append(diff)
        flux = times(coeff, diff)
        flux_dot = times(slope, diff)
        if main_dot is not None:
            diff_dot = faces(main_dot, edge_dot, False)
            flux_dot = plus(flux_dot, times(coeff, diff_dot))
        else:
            diff_dot = None
        diffs_dot.append(diff_dot)
        spread_m, spread_e = gathered(flux, reach, False)
        dot_m, dot_e = gathered(flux_dot, reach, False)
        new = [{}, {}, {}, {}]
        for kind, table, old, old_dot, spread, dot in (
            (0, FWD_MAIN, main, main_dot, spread_m, dot_m),
            (1, FWD_EDGE, edge, edge_dot, spread_e, dot_e),
        ):
            for dx in spread:
                n = spread[dx].shape[0]
                new[kind][dx] = old[dx][:n] + mixed(fwd, table[dx], spread[dx])
                moved = mixed(fwd, table[dx], dot[dx])
                new[2 + kind][dx] = moved if old_dot is None else old_dot[dx][:n] + moved
        main, edge, main_dot, edge_dot = new

    obs = jnp.concatenate([obs_v[s] for s in range(SPECIES)] + [jnp.zeros((ROWS - SPECIES, LANES), jnp.float32)], 0)
    miss = main[0].reshape(ROWS, LANES) - obs
    miss_dot = main_dot[0].reshape(ROWS, LANES)
    square_sum = jnp.sum(miss * miss, 0, keepdims=True)
    cross_sum = jnp.sum(miss * miss_dot, 0, keepdims=True)
    front = lane((1, LANES)) < LANES // 2
    half_row = LANES // 2
    part = jnp.where(front, square_sum + spin(square_sum, half_row), cross_sum + spin(cross_sum, half_row))
    part_out[0] = part
    pl.semaphore_wait(ready, 4 - direct.astype(jnp.int32))

    def straight(across, mid):
        north, east = across // 4, across % 4
        offset = (north - x_hi + 4) % 4 * 4 + (east - y_lo + 4) % 4

        @pl.when(offset > 0)
        def _():
            for core in (1, 0):
                step = (core + x_core) % 2 + (mid - x_mid + 4) % 4 * 2 + y_hi * 8
                partner = north * 8 + mid * 2 + core, jnp.int32(east)
                part_copy(2, part_all.at[offset * 16 - 1 + step], partner).start()

    def along_z(height):
        high, mid = height // 4, height % 4
        for core in (1, 0):
            step = (core + x_core) % 2 + (mid - x_mid + 4) % 4 * 2 + (high + y_hi) % 2 * 8

            @pl.when(step > 0)
            def _(core=core, step=step):
                partner = x_hi * 8 + mid * 2 + core, high * 4 + y_lo
                part_copy(0, part_all.at[step - 1], partner).start()

    straight(0, 0)
    for across in range(4):
        straight(across, 1)
    for height in range(8):
        along_z(height)
    for across in range(1, 16):
        straight(across, 0)
    for across in range(4, 16):
        straight(across, 1)

    shared = miss[8:] + pltpu.roll(miss_dot[8:], 4, 0)
    tiles = [miss[:8], miss_dot[:8], shared]
    for i, tile in enumerate(tiles):
        rim_out[i * 8 : i * 8 + 8] = tile
    rim_strip[0], rim_strip[1] = fold_strips(pack_strips(tiles))
    neighbours(lambda *place: rim_copy(*place).start())

    for dx, column in ADJ_MAIN.items():
        select_table(adj, column, adj_parts, soil_m[dx])
    for dx, column in ADJ_EDGE.items():
        select_table(adj, column, adj_parts, soil_e[dx])

    near, far = part_all.at[pl.ds(0, 15)], part_all.at[pl.ds(15, 240)]

    def all_arrived(buffer, index):
        pltpu.make_async_copy(buffer, buffer, recv_sem.at[2 * len(SEM) + index]).wait()

    @pl.when(jnp.logical_not(direct))
    def _():
        all_arrived(near, 0)
        part_out[1] = part + jnp.sum(part_all[0:15], 0)
        for slot, partner in enumerate(group_b):
            part_copy(1, part_b.at[slot], partner).start()

    arrived(rim_copy)
    lam_m, lam_e, mu_m, mu_e = {}, {}, {}, {}

    def rim_fields(tiles):
        fields = jnp.stack([tiles[0], tiles[2], tiles[1], pltpu.roll(tiles[2], 4, 0)])
        fields = fields.reshape(2, 2, 8, LANES)
        return fields[:1], fields[1:]

    for dx in range(-STEPS, STEPS + 1):
        own = [rim[pl.ds(RIM[dx] + i * 8, 8)] for i in range(3)] if dx else tiles
        lam_m[dx], mu_m[dx] = rim_fields(own)
        if abs(dx) < STEPS:
            left, right = unfold_strips(rim_y[STRIP[dx, -1]], rim_y[STRIP[dx, 1]])
            lam_e[dx], mu_e[dx] = rim_fields([unpack_strip(left, right, i) for i in range(3)])

    sums = {}

    def into(key, value):
        value = value[:, 0] + value[:, 1]
        if key in sums:
            old = sums[key]
            n = old.shape[0]
            sums[key] = jnp.concatenate([old + value[:n], value[n:]], 0) if value.shape[0] > n else old + value
        else:
            sums[key] = value

    own = (("xm", 0), ("xm", -1), ("zm", 0), ("ym", 0), ("ye", 0))
    for k in reversed(range(STEPS)):
        reach = STEPS - 1 - k
        u_m = {dx: mixed(adj, ADJ_MAIN[dx], lam_m[dx]) for dx in lam_m}
        v_m = {dx: mixed(adj, ADJ_MAIN[dx], mu_m[dx]) for dx in mu_m}
        u_e = {dx: mixed(adj, ADJ_EDGE[dx], lam_e[dx]) for dx in lam_e}
        v_e = {dx: mixed(adj, ADJ_EDGE[dx], mu_e[dx]) for dx in mu_e}
        diff_u, diff_v = faces(u_m, u_e, True), faces(v_m, v_e, True)
        for key in own:
            du, dv, dc = diff_u[key], diff_v[key], diffs[k][key][: diff_u[key].shape[0]]
            into(("g", key), du * dc)
            second = dv * dc
            if diffs_dot[k] is not None:
                second = second + du * diffs_dot[k][key][: du.shape[0]]
            into(("h", key), second)
        if k == 0:
            break
        need = lambda diff: {
            key: value for key, value in diff.items()
            if key[0][0] == "x" or abs(key[1]) <= (k if key[0] != "ze" else k - 1)
        }
        diff_u, diff_v = need(diff_u), need(diff_v)
        step_m, step_e = gathered(times(coeff, diff_u), k, True)
        dot_m, dot_e = gathered(plus(times(coeff, diff_v), times(slope, diff_u)), k, True)

        def added(old, step):
            n = old.shape[0]
            return jnp.concatenate([old + step[:n], step[n:]], 0)

        lam_m, lam_e = (
            {dx: added(lam_m[dx], step_m[dx]) for dx in step_m},
            {dx: added(lam_e[dx], step_e[dx]) for dx in step_e},
        )
        mu_m, mu_e = (
            {dx: added(mu_m[dx], dot_m[dx]) for dx in dot_m},
            {dx: added(mu_e[dx], dot_e[dx]) for dx in dot_e},
        )

    def per_cell(name):
        y_sum = sums[name, ("ym", 0)]
        side = sums[name, ("xm", 0)] + sums[name, ("xm", -1)] + y_sum
        side = side + y_prev(y_sum, sums[name, ("ye", 0)])[0]
        depth = sums[name, ("zm", 0)]
        n = side.shape[0]
        total = jnp.concatenate([side + depth[:n] + depth[1:], depth[n:]], 0)
        return jnp.sum(total, 1, keepdims=True)

    weight = weight_m[0][:, 0, :1, :]
    plain_part = -weight * per_cell("g")
    dot_part = -weight * per_cell("h") + own_dire[:, 0, :1, :] * plain_part

    neighbours(lambda *place: halo_copy(*place).wait_send())
    neighbours(lambda *place: rim_copy(*place).wait_send())
    def all_sent(buffer, index):
        pltpu.make_async_copy(buffer, buffer, send_sem.at[2 * len(SEM) + index]).wait()

    all_sent(near, 0)
    all_sent(part_all.at[pl.ds(0, 60)], 2)

    @pl.when(direct)
    def _():
        all_arrived(near, 0)
        close = part_out[0] + jnp.sum(part_all[0:15], 0)
        all_arrived(far, 2)
        rest = part_all[15:255].reshape(30, 8, 1, LANES)
        part_sum[...] = close + jnp.sum(jnp.sum(rest, 0), 0)

    @pl.when(jnp.logical_not(direct))
    def _():
        all_sent(part_b, 1)
        all_arrived(part_b, 1)
        part_sum[...] = part_out[1] + jnp.sum(part_b[...], 0)

    part = part_sum[...]
    total = jnp.sum(jnp.where(front, part, 0.0), 1, keepdims=True)
    cross = jnp.sum(jnp.where(front, 0.0, part), 1, keepdims=True)
    count = float(SPECIES * nx * ny * LANES)
    factor = count / total
    second = -2.0 * count * cross / (total * total)
    zero = jnp.zeros((1, LANES), jnp.float32)
    for z in range(16):
        one, two = (dot_part[z], plain_part[z]) if z <= STEPS else (zero, zero)
        out_ref[0, z : z + 1, :] = factor * one + second * two


def solution(mesh):
    nx, ny = mesh.shape["gx"], mesh.shape["gy"]

    def body(c_start, log_tort, direction, mix_inverse, pair_mask, soil_layer, observed):
        f32 = jnp.float32
        hbm = pl.BlockSpec(memory_space=pltpu.HBM)
        vmem = pl.BlockSpec(memory_space=pltpu.VMEM)
        return pl.pallas_call(
            lambda *refs: kernel(nx, ny, *refs),
            out_shape=jax.ShapeDtypeStruct((1, 16, LANES), f32),
            in_specs=[hbm] * 7,
            out_specs=vmem,
            scratch_shapes=[
                pltpu.VMEM((ROWS + 1, 8, LANES), f32),
                pltpu.VMEM((1, LANES), jnp.int32),
                pltpu.VMEM((SPECIES, 1, LANES), f32),
                pltpu.VMEM((SPECIES, LAYERS, SPECIES), f32),
                pltpu.VMEM((SPECIES, SPECIES), jnp.int32),
                pltpu.VMEM(((STEPS + 1) * ROWS, LANES), f32),
                pltpu.VMEM((2, 4, LANES), f32),
                pltpu.VMEM((HALO_ROWS, LANES), f32),
                pltpu.VMEM((len(ACROSS), 4, LANES), f32),
                pltpu.VMEM((RIM_ROWS, LANES), f32),
                pltpu.VMEM((2, 4, LANES), f32),
                pltpu.VMEM((len(ALONG_X) * RIM_ROWS, LANES), f32),
                pltpu.VMEM((len(ACROSS), 4, LANES), f32),
                pltpu.VMEM((2, 1, LANES), f32),
                pltpu.VMEM((255, 1, LANES), f32),
                pltpu.VMEM((15, 1, LANES), f32),
                pltpu.VMEM((1, LANES), f32),
                pltpu.VMEM((LANES, LANES), f32),
                pltpu.VMEM((LAYERS, SPECIES, 2, 8, LANES), f32),
                pltpu.VMEM((LAYERS, SPECIES, 2, 8, LANES), f32),
                pltpu.VMEM((8, SPECIES, 2, 8, LANES), f32),
                pltpu.VMEM((12, SPECIES, 2, 8, LANES), f32),
                pltpu.SemaphoreType.DMA((7,)),
                pltpu.SemaphoreType.DMA((2 * len(SEM) + 3,)),
                pltpu.SemaphoreType.DMA((2 * len(SEM) + 3,)),
                pltpu.SemaphoreType.REGULAR,
            ],
            compiler_params=pltpu.CompilerParams(
                collective_id=0, has_side_effects=True, vmem_limit_bytes=32 * 1024 * 1024
            ),
        )(*(
            pltpu.with_memory_space_constraint(value, pltpu.HBM)
            for value in (
                c_start, log_tort, direction, mix_inverse.transpose(1, 0, 2), pair_mask, soil_layer, observed,
            )
        ))

    return jax.shard_map(
        body,
        mesh=mesh,
        in_specs=(
            P(None, "gx", None, "gy"),
            P("gx", None, "gy"),
            P("gx", None, "gy"),
            P(),
            P(),
            P("gx", "gy"),
            P(None, "gx", "gy"),
        ),
        out_specs=P("gx", None, "gy"),
        check_vma=False,
    )
```
